32 devices in a mesh: graph: 8 (over z, core), replica: 4 (over y, x).
Axes of the slice: x: 2, y: 2, z: 4, core: 2. Of those that a mesh axis runs over, the one named last changes fastest.
Arguments:
- features: bfloat16 [4, 1024, 512], P('replica', 'graph'), may hold values from -8 to 8
- neighbours: int32 [4, 1024, 16], P('replica', 'graph'), may hold values from 0 to 143
- send_rows: int32 [4, 8, 8, 2], P('replica', 'graph'), may hold values from 0 to 127
- send_counts: int32 [4, 8, 8], P('replica', 'graph'), may hold values from 0 to 2, as said below
- candidates: int32 [4, 256, 512], P('replica', 'graph'), may hold values from 0 to 127
- perturbation: float32 [4, 256, 4, 512], P('replica', 'graph'), may hold values from -320 to 320
- weight: bfloat16 [512, 512], replicated, may hold values from -0.25 to 0.25
Outputs:
- d_features: bfloat16 [4, 1024, 512], P('replica', 'graph')
- weight_grad: float32 [512, 512], P('graph', 'replica')
The draws below stay inside these ranges and needn't reach their ends.
Inputs may be any that keep to these rules, and one draw needn't show every extreme that they name: `send_counts`: rows that one device sends to another in its mini-batch; in every draw one device of each mini-batch receives 2 rows from every device.
All inputs are finite; a program needn't handle non-finite values.
Results may differ from the reference program's by a relative error of at most 0.013.
Values may be sent and summed in bfloat16 or wider, within the bound.
No kernel may reach another device: no remote copies, remote signals or barrier semaphores. Data moves between devices by JAX's collectives and lax.ppermute only.
A program may use at most 64 MiB of HBM per device.

```python
import math
import jax
import jax.numpy as jnp
from jax import lax

D = 512
NODE_DEV = 128
CAP = 2
FANOUT = 16
CANDS = 512
TOP = 20
SAMPLES = 4
QUERY_DEV = 32
NODES = 1024
QUERIES = 256
N_GRAPH = 8
N_REPLICA = 4


def draw_features(key, part):
    key = jax.random.fold_in(key, 11)
    first = jax.random.fold_in(key, 0)
    shape = (N_REPLICA, N_GRAPH * NODE_DEV, D)
    return jnp.clip(jax.random.normal(first, shape, jnp.float32), -6.0, 6.0).astype(jnp.bfloat16)


def draw_send_counts(key, part):
    key = jax.random.fold_in(key, 23)
    first, second, third = jax.random.split(key, 3)
    heat = jax.random.randint(first, (N_REPLICA, N_GRAPH, 1), 1, 5)
    ceiling = CAP * heat // 4
    counts = jax.random.randint(second, (N_REPLICA, N_GRAPH, N_GRAPH), 0, ceiling + 1)
    busiest = jax.random.randint(third, (N_REPLICA, 1, 1), 0, N_GRAPH)
    receiver = jnp.arange(N_GRAPH, dtype=jnp.int32)[None, :, None]
    return jnp.where(receiver == busiest, CAP, counts).astype(jnp.int32)


def draw_perturbation(key, part):
    key = jax.random.fold_in(key, 37)
    keys = jax.random.split(key, 1)
    shape = (N_REPLICA, N_GRAPH * QUERY_DEV, SAMPLES, CANDS)
    return jnp.clip(jax.random.normal(keys[0], shape, jnp.float32), -6.0, 6.0)


def set_ends(drawn, rng, smallest, high):
    longest = drawn.shape.index(max(drawn.shape))
    spots = []
    for shift in (0, 1):
        where = [jax.random.randint(jax.random.fold_in(rng, axis), (), 0, length) for axis, length in enumerate(drawn.shape)]
        where[longest] = (where[longest] + shift) % drawn.shape[longest]
        spots.append(tuple(where))
    return drawn.at[spots[0]].set(smallest).at[spots[1]].set(high)


def normal_values(rng, shape, width, limit, kind=jnp.bfloat16):
    return jnp.clip(width * jax.random.normal(rng, shape, jnp.float32), -limit, limit).astype(kind)


def setup_inputs(seed: int = 0) -> dict:
    seeds = jax.random.split(jax.random.key(seed), 8)
    return {
        "features": draw_features(jax.random.fold_in(seeds[7], 71), 0),
        "neighbours": set_ends(jax.random.randint(seeds[1], (N_REPLICA, NODES, FANOUT), 0, NODE_DEV + N_GRAPH * CAP), jax.random.fold_in(seeds[1], 1), 0, (NODE_DEV + N_GRAPH * CAP) - 1).astype(jnp.int32),
        "send_rows": set_ends(jax.random.randint(seeds[2], (N_REPLICA, N_GRAPH, N_GRAPH, CAP), 0, NODE_DEV), jax.random.fold_in(seeds[2], 1), 0, NODE_DEV - 1).astype(jnp.int32),
        "send_counts": draw_send_counts(jax.random.fold_in(seeds[7], 71), 0),
        "candidates": set_ends(jax.random.randint(seeds[4], (N_REPLICA, QUERIES, CANDS), 0, NODE_DEV), jax.random.fold_in(seeds[4], 1), 0, NODE_DEV - 1).astype(jnp.int32),
        "perturbation": draw_perturbation(jax.random.fold_in(seeds[7], 71), 0),
        "weight": normal_values(seeds[6], (D, D), D ** -0.5, 0.25),
    }


SCORE_SCALE = 16.0
LOSS_SCALE = 16.0
EPSILON = 1e-05

def embed_backward(mean_rows, weight, candidates, perturbation):
    query_count = candidates.shape[0]
    pre = jnp.dot(mean_rows, weight, preferred_element_type=jnp.float32)
    inverse = lax.rsqrt(lax.optimization_barrier(jnp.mean(pre * pre, axis=-1, keepdims=True)) + EPSILON)
    embedded = (pre * inverse).astype(jnp.bfloat16)
    similar = jnp.dot(embedded[:query_count], embedded.T, preferred_element_type=jnp.float32)
    factor = SCORE_SCALE / pre.shape[1]
    scores = factor * jnp.take_along_axis(similar, candidates, axis=1)
    perturbed = scores[:, None, :] + perturbation
    highest = lax.optimization_barrier(jnp.max(perturbed, axis=-1, keepdims=True))
    exponent = jnp.exp(perturbed - highest)
    weights_soft = exponent / lax.optimization_barrier(jnp.sum(exponent, axis=-1, keepdims=True))
    target = (jnp.arange(candidates.shape[1], dtype=jnp.int32) < TOP).astype(jnp.float32)
    d_scores = LOSS_SCALE * (TOP * lax.optimization_barrier(jnp.mean(weights_soft, axis=1)) - target[None, :])
    query_index = jnp.broadcast_to(jnp.arange(query_count, dtype=jnp.int32)[:, None], candidates.shape)
    d_similar = jnp.zeros((query_count, embedded.shape[0]), jnp.float32).at[query_index, candidates].add(d_scores).astype(jnp.bfloat16)
    d_embedded = factor * lax.dot_general(d_similar, embedded[:query_count], (((0,), (0,)), ((), ())), preferred_element_type=jnp.float32)
    d_queries = factor * jnp.dot(d_similar, embedded, preferred_element_type=jnp.float32)
    d_embedded = d_embedded.at[:query_count].add(d_queries)
    d_pre = inverse * d_embedded - inverse * inverse * inverse * pre * lax.optimization_barrier(jnp.mean(d_embedded * pre, axis=-1, keepdims=True))
    return d_pre.astype(jnp.bfloat16)

def device_pass(feature_rows, halo, keep, neighbour_rows, candidate_rows, noise_rows, weight):
    row_count = feature_rows.shape[0]
    table = jnp.concatenate([feature_rows, halo], axis=0)
    total = feature_rows.astype(jnp.float32) + lax.optimization_barrier(jnp.sum(table[neighbour_rows].astype(jnp.float32), axis=1))
    mean_rows = (total / (FANOUT + 1)).astype(jnp.bfloat16)
    d_pre = embed_backward(mean_rows, weight, candidate_rows, noise_rows)
    term = lax.dot_general(mean_rows, d_pre, (((0,), (0,)), ((), ())), preferred_element_type=jnp.float32)
    share = (jnp.dot(d_pre, weight.T, preferred_element_type=jnp.float32) / (FANOUT + 1)).astype(jnp.bfloat16)
    share_wide = share.astype(jnp.float32)
    spread = jnp.broadcast_to(share_wide[:, None, :], neighbour_rows.shape + (share.shape[1],))
    d_table = jnp.zeros(table.shape, jnp.float32).at[neighbour_rows].add(spread)
    d_local = share_wide + d_table[:row_count]
    halo_grad = jnp.where(keep[:, None], d_table[row_count:], 0.0).astype(jnp.bfloat16)
    return (d_local, halo_grad, term)

def reference(features, neighbours, send_rows, send_counts, candidates, perturbation, weight):
    feature_grid = features.reshape(N_REPLICA, N_GRAPH, NODE_DEV, D)
    neighbour_grid = neighbours.reshape(N_REPLICA, N_GRAPH, NODE_DEV, FANOUT)
    candidate_grid = candidates.reshape(N_REPLICA, N_GRAPH, QUERY_DEV, CANDS)
    noise_grid = perturbation.reshape(N_REPLICA, N_GRAPH, QUERY_DEV, SAMPLES, CANDS)
    source = jnp.arange(N_GRAPH, dtype=jnp.int32)[:, None]
    slots = jnp.arange(CAP, dtype=jnp.int32)[None, :]

    def replica_step(w_total, pieces):
        feature_rep, neighbour_rep, send_rep, count_rep, candidate_rep, noise_rep = pieces

        def device_step(w_sum, inner):
            position, neighbour_rows, candidate_rows, noise_rows, counts = inner
            rows_from = send_rep[:, position, :]
            keep = slots < counts[:, None]
            halo = jnp.where(keep[:, :, None], feature_rep[source, rows_from], jnp.zeros((), jnp.bfloat16))
            d_local, halo_grad, term = device_pass(feature_rep[position], halo.reshape(N_GRAPH * CAP, D), keep.reshape(-1), neighbour_rows, candidate_rows, noise_rows, weight)
            return (w_sum + term, (d_local, halo_grad))
        positions = jnp.arange(N_GRAPH, dtype=jnp.int32)
        w_total, (d_local, halo_grad) = lax.scan(device_step, w_total, (positions, neighbour_rep, candidate_rep, noise_rep, count_rep))
        returned = halo_grad.reshape(N_GRAPH, N_GRAPH, CAP, D).transpose(1, 0, 2, 3).astype(jnp.float32)
        d_rep = d_local.at[source[:, :, None], send_rep].add(returned)
        return (w_total, d_rep.astype(jnp.bfloat16))
    w_total, d_all = lax.scan(replica_step, jnp.zeros((D, D), jnp.float32), (feature_grid, neighbour_grid, send_rows, send_counts, candidate_grid, noise_grid))
    weight_grad = w_total / math.sqrt(N_GRAPH * N_REPLICA)
    return (d_all.reshape(N_REPLICA, NODES, D), weight_grad)
```

```python
import functools
import math

import jax
import jax.numpy as jnp
from jax import lax
from jax.experimental import pallas as pl
from jax.experimental.pallas import tpu as pltpu
from jax.sharding import PartitionSpec as P

TOP = 20
SCORE_SCALE = 16.0
LOSS_SCALE = 16.0
EPSILON = 1e-05
LANES = 128
DIGIT = 16
F32 = jnp.float32
BF16 = jnp.bfloat16
NN = (((1,), (0,)), ((), ()))
TN = (((0,), (0,)), ((), ()))
NT = (((1,), (1,)), ((), ()))


def dot(a, b, dims):
    return lax.dot_general(a, b, dims, preferred_element_type=F32)


def slot_device(slot, towers):
    core = lax.axis_index("core")
    pair, e = slot // 2, slot % 2
    mixed = jnp.where(pair > 1, 1, 0)
    odd = pair % 2 * mixed
    upper = pair % 2 * (1 - mixed) + lax.bitwise_xor(core, odd) * mixed
    z = lax.bitwise_xor(lax.axis_index("z"), pair // 2 + upper * (towers // 2))
    return 2 * z + lax.bitwise_xor(core, lax.bitwise_xor(odd, jnp.int32(e)))


def kept_slots(towers):
    return [0, 2] + [4 * j + e for j in range(1, towers // 2) for e in range(2)]


def sent_slots(towers):
    return [1, 3] + [4 * j + 2 + e for j in range(1, towers // 2) for e in range(2)]


def slot_tiles(tiles):
    core = lax.axis_index("core")
    pairs = [xor_order(tiles[2 * z : 2 * z + 2], core) for z in range(len(tiles) // 2)]
    same = xor_order([pair[0] for pair in pairs], lax.axis_index("z"))
    other = xor_order([pair[1] for pair in pairs], lax.axis_index("z"))
    half = len(pairs) // 2
    ordered = [same[0], other[0], same[half], other[half]]
    for j in range(1, half):
        first = [xor_order([found[j], found[half + j]], core) for found in (same, other)]
        ordered += [first[0][0], first[1][0], first[1][1], first[0][1]]
    return ordered


def pick(array, slots, size):
    return jnp.concatenate([array[i * size : (i + 1) * size] for i in slots], axis=0)


def fold(rows):
    return jnp.concatenate(
        [rows[:, j : j + LANES] for j in range(0, rows.shape[1], LANES)], axis=0
    )


def unfold(block, parts):
    size = block.shape[0] // parts
    return jnp.concatenate([block[j * size : (j + 1) * size] for j in range(parts)], axis=1)


def near_rows(kept, arrived, size):
    return jnp.concatenate([pick(kept, [1], size), pick(arrived, [1], size)], axis=0)


def far_rows(kept, arrived, j, size):
    return jnp.concatenate([pick(x, [2 * j, 2 * j + 1], size) for x in (kept, arrived)], axis=0)


def slot_rows(kept, arrived, near, far, passed, size):
    rows = [pick(kept, [0], size), pick(arrived, [0], size), near]
    for j, block in enumerate(far):
        rows += [pick(block, [0, 2], size), pick(passed, [2 * j, 2 * j + 1], size)]
    return jnp.concatenate(rows, axis=0)


def xor_order(pieces, me):
    bit = 1
    while bit < len(pieces):
        swap = lax.bitwise_and(me, jnp.int32(bit)) != 0
        pieces = [jnp.where(swap, pieces[i ^ bit], pieces[i]) for i in range(len(pieces))]
        bit *= 2
    return pieces


def start_copies(pairs, sems):
    copies = [pltpu.make_async_copy(a, b, sems.at[i]) for i, (a, b) in enumerate(pairs)]
    for copy in copies:
        copy.start()
    return copies


def outgoing_kernel(
    towers,
    capacity,
    send_hbm,
    counts_hbm,
    features_hbm,
    neighbours_hbm,
    kept_ref,
    sent_ref,
    onehot_ref,
    held_ref,
    features_ref,
    neighbours_ref,
    send_smem,
    counts_smem,
    sems,
):
    copies = start_copies(
        [
            (send_hbm, send_smem),
            (counts_hbm, counts_smem),
            (features_hbm, features_ref),
            (neighbours_hbm, neighbours_ref),
        ],
        sems,
    )
    rows = features_ref.shape[0]
    slots = 2 * towers * capacity
    slot = lax.broadcasted_iota(jnp.int32, (slots, rows), 0)
    row = lax.broadcasted_iota(jnp.int32, (slots, rows), 1)
    named = jnp.full((slots, rows), -1, jnp.int32)
    held = jnp.zeros((slots, rows), jnp.int32)
    copies[0].wait()
    copies[1].wait()
    for i in range(2 * towers):
        device = slot_device(i, towers)
        held = jnp.where(slot // capacity == i, counts_smem[0, device], held)
        for k in range(capacity):
            named = jnp.where(slot == i * capacity + k, send_smem[k, device], named)
    onehot = (named == row).astype(F32).astype(BF16)
    onehot_ref[...] = onehot
    held_ref[...] = (slot % capacity < held).astype(F32)
    copies[2].wait()
    picked = dot(onehot, features_ref[...], NN)
    kept_ref[...] = pick(picked, kept_slots(towers), capacity)
    sent_ref[...] = pick(picked, sent_slots(towers), capacity)
    copies[3].wait()


def hop_kernel(capacity, after_ref, kept_ref, arrived_ref, near_ref, *far_refs):
    kept, arrived = kept_ref[...], arrived_ref[...]
    near_ref[...] = near_rows(kept, arrived, capacity).astype(BF16)
    for j, ref in enumerate(far_refs):
        ref[...] = far_rows(kept, arrived, j + 1, capacity).astype(BF16)


def pass_kernel(capacity, *refs):
    far_refs, out_ref = refs[:-1], refs[-1]
    rows = [pick(ref[...].astype(F32), [1, 3], capacity) for ref in far_refs]
    out_ref[...] = jnp.concatenate(rows, axis=0).astype(BF16)


def adjacency_kernel(
    towers,
    capacity,
    held_ref,
    features_ref,
    neighbours_ref,
    own_ref,
    far_ref,
    far_turned_ref,
    start_ref,
):
    rows = features_ref.shape[0]
    fanout = neighbours_ref.shape[0]
    slots = far_ref.shape[0]
    own = lax.broadcasted_iota(jnp.int32, (rows, rows), 0)
    far = lax.broadcasted_iota(jnp.int32, (slots, rows), 0)
    far_slot = slot_device(far // capacity, towers) * capacity + far % capacity + rows
    own_count = jnp.zeros((rows, rows), F32)
    far_count = jnp.zeros((slots, rows), F32)
    for f in range(fanout):
        named = neighbours_ref[f : f + 1, :]
        own_count = own_count + (own == named).astype(F32)
        far_count = far_count + (far_slot == named).astype(F32)
    own_count = own_count.astype(BF16)
    far_count = far_count * held_ref[...]
    far_ref[...] = far_count.astype(BF16)
    far_turned_ref[...] = far_count.T.astype(BF16)
    own_ref[...] = own_count
    features = features_ref[...]
    start_ref[...] = features.astype(F32) + dot(own_count, features, TN)


def prepare_kernel(
    candidates_hbm,
    noise_hbm,
    weight_hbm,
    candidates_ref,
    noise_ref,
    weight_ref,
    marks_ref,
    raw_noise_ref,
    sems,
):
    copies = start_copies(
        [(candidates_hbm, candidates_ref), (noise_hbm, raw_noise_ref), (weight_hbm, weight_ref)], sems
    )
    queries, cands = candidates_ref.shape
    blocks = cands // LANES
    samples = noise_ref.shape[0] // (queries * blocks)
    copies[0].wait()
    low = lax.bitwise_and(candidates_ref[...], jnp.int32(DIGIT - 1))
    for digit in range(DIGIT):
        marks_ref[digit * queries : (digit + 1) * queries, :] = (
            (low == digit).astype(F32).astype(BF16)
        )
    copies[1].wait()
    for m in range(samples):
        noise = [
            raw_noise_ref[pl.ds(j * samples + m, queries, stride=blocks * samples), :]
            for j in range(blocks)
        ]
        highest = jnp.max(functools.reduce(jnp.maximum, noise), axis=-1, keepdims=True)
        for j in range(blocks):
            at = (m * blocks + j) * queries
            noise_ref[at : at + queries, :] = jnp.exp(noise[j] - highest)
    copies[2].wait()


def main_kernel(
    towers,
    capacity,
    fanout,
    far_turned_ref,
    start_ref,
    candidates_ref,
    noise_ref,
    weight_ref,
    marks_ref,
    halo_kept_ref,
    halo_arrived_ref,
    *refs,
):
    *halo_refs, kept_turned_ref, sent_ref, d_pre_ref = refs
    *far_halo, passed, near = [ref[...].astype(F32) for ref in halo_refs]
    rows, width = start_ref.shape
    queries, cands = candidates_ref.shape
    samples = noise_ref.shape[0] // (queries * (cands // LANES))
    halo = slot_rows(halo_kept_ref[...], halo_arrived_ref[...], near, far_halo, passed, capacity)
    sums = start_ref[...] + dot(far_turned_ref[...], halo.astype(BF16), NN)
    mean_rows = (sums * (1.0 / (fanout + 1))).astype(BF16)

    tall = width // (2 * towers)
    turned = mean_rows.astype(F32).T
    tiles = slot_tiles([turned[i * tall : (i + 1) * tall] for i in range(2 * towers)])
    kept_turned, sent_turned = [
        jnp.concatenate([tiles[i] for i in slots], axis=0).astype(BF16)
        for slots in (kept_slots(towers), sent_slots(towers))
    ]

    weight = weight_ref[...]
    pre = dot(mean_rows, weight, NN)
    inverse = lax.rsqrt(jnp.mean(pre * pre, axis=-1, keepdims=True) + EPSILON)
    embedded = (pre * inverse).astype(BF16)
    factor = SCORE_SCALE / width
    rounded = pre.astype(BF16)
    similar = dot(rounded[:queries], rounded, NT)
    inverse_of_column = jnp.broadcast_to(inverse, (rows, rows)).T[:queries]
    similar = similar * (factor * inverse[:queries] * inverse_of_column)
    blocks = cands // LANES
    scores = [
        jnp.take_along_axis(similar, candidates_ref[:, j * LANES : (j + 1) * LANES], axis=1)
        for j in range(blocks)
    ]
    grown = [jnp.exp(x) for x in scores]
    soft = [jnp.zeros((queries, LANES), F32) for _ in range(blocks)]
    for m in range(samples):
        at = m * blocks * queries
        noise = [noise_ref[at + j * queries : at + (j + 1) * queries, :] for j in range(blocks)]
        total = jnp.sum(sum(n * g for n, g in zip(noise, grown)), axis=-1, keepdims=True)
        scale = (LOSS_SCALE * TOP / samples) / total
        soft = [a + n * scale for a, n in zip(soft, noise)]
    soft = [a * g for a, g in zip(soft, grown)]
    lane = lax.broadcasted_iota(jnp.int32, (queries, LANES), 1)
    d_scores = [
        jnp.where(lane + j * LANES < TOP, s - LOSS_SCALE, s) if j * LANES < TOP else s
        for j, s in enumerate(soft)
    ]
    d_scores = jnp.concatenate(d_scores, axis=1)

    high = candidates_ref[...] // DIGIT
    digits = rows // DIGIT
    weighted = [jnp.where(high == digit, d_scores, 0.0) for digit in range(digits)]
    crossed = dot(marks_ref[...], jnp.concatenate(weighted, axis=0).astype(BF16), NT)
    q_row = lax.broadcasted_iota(jnp.int32, crossed.shape, 0) % queries
    q_column = lax.broadcasted_iota(jnp.int32, crossed.shape, 1) % queries
    crossed = jnp.where(q_row == q_column, crossed, 0.0)
    kept = jnp.sum(crossed.reshape(DIGIT, queries, digits * queries), axis=1)
    d_similar = jnp.concatenate(
        [kept[:, i * queries : (i + 1) * queries] for i in range(digits)], axis=0
    ).astype(BF16)

    d_embedded = factor * dot(d_similar, embedded[:queries], NN)
    d_queries = factor * dot(d_similar, embedded, TN)
    d_embedded = jnp.concatenate(
        [d_embedded[:queries] + d_queries, d_embedded[queries:]], axis=0
    )
    inner = jnp.mean(d_embedded * pre, axis=-1, keepdims=True)
    d_pre = (inverse * d_embedded - inverse * inverse * inverse * pre * inner).astype(BF16)

    d_pre_ref[...] = d_pre
    sent_ref[...] = dot(sent_turned, d_pre, NN).astype(BF16)
    kept_turned_ref[...] = kept_turned


def own_term_kernel(kept_turned_ref, d_pre_ref, out_ref):
    out_ref[...] = dot(kept_turned_ref[...], d_pre_ref[...], NN)


def spread_kernel(
    towers, capacity, fanout, d_pre_ref, weight_ref, own_ref, far_ref, local_ref, kept_ref, sent_ref
):
    share = (dot(d_pre_ref[...], weight_ref[...], NT) * (1.0 / (fanout + 1))).astype(BF16)
    halo_grad = dot(far_ref[...], share, NN)
    kept_ref[...] = pick(halo_grad, kept_slots(towers), capacity)
    sent_ref[...] = pick(halo_grad, sent_slots(towers), capacity)
    local_ref[...] = share.astype(F32) + dot(own_ref[...], share, NN)


def core_sum_kernel(replicas, kept_ref, arrived_ref, own_ref, *out_refs):
    total = kept_ref[...] + arrived_ref[...].astype(F32)
    wide = total.shape[1] // replicas
    pieces = [total[:, r * wide : (r + 1) * wide] for r in range(replicas)]
    pieces = xor_order(pieces, lax.axis_index("replica"))
    own_ref[...] = pieces[0]
    for ref, piece in zip(out_refs, pieces[:0:-1]):
        ref[...] = piece.astype(BF16)


def store_block(ref, tiles, rows):
    high, wide = tiles.shape
    block = fold(rows)
    if (high + block.shape[0], wide) != ref.shape:
        ref[...] = jnp.zeros(ref.shape, ref.dtype)
    ref[0:high, 0:wide] = tiles.astype(ref.dtype)
    ref[ref.shape[0] - block.shape[0] :, :] = block.astype(ref.dtype)


def load_block(ref, high, wide, slots, parts):
    block = ref[...].astype(F32)
    return block[:high, :wide], unfold(block[block.shape[0] - slots * parts :], parts)


def replica_sum_kernel(replicas, capacity, *refs):
    term_refs, refs = refs[:replicas], refs[replicas:]
    kept_ref, arrived_ref, own_ref, near_ref, *far_refs = refs
    total = sum(ref[...].astype(F32) for ref in term_refs)
    tall = own_ref.shape[0]
    kept, arrived = kept_ref[...], arrived_ref[...]
    own_ref[...] = total[:tall]
    store_block(near_ref, total[tall : 2 * tall], near_rows(kept, arrived, capacity))
    for j, ref in enumerate(far_refs):
        tiles = total[2 * (j + 1) * tall : 2 * (j + 2) * tall]
        store_block(ref, tiles, far_rows(kept, arrived, j + 1, capacity))


def pass_sums_kernel(capacity, parts, tall, wide, *refs):
    far_refs, out_ref = refs[:-1], refs[-1]
    loaded = [load_block(ref, 2 * tall, wide, 4 * capacity, parts) for ref in far_refs]
    store_block(
        out_ref,
        sum(tiles[tall:] for tiles, _ in loaded),
        jnp.concatenate([pick(rows, [1, 3], capacity) for _, rows in loaded], axis=0),
    )


def final_kernel(capacity, devices, local_ref, onehot_ref, kept_ref, arrived_ref, own_ref, *refs):
    *far_refs, passed_ref, near_ref, features_out, weight_out = refs
    tall, wide = own_ref.shape
    parts = local_ref.shape[1] // LANES
    near_tile, near = load_block(near_ref, tall, wide, 2 * capacity, parts)
    loaded = [load_block(ref, 2 * tall, wide, 4 * capacity, parts) for ref in far_refs]
    passed_tile, passed = load_block(passed_ref, tall, wide, 2 * capacity * len(far_refs), parts)
    returned = slot_rows(
        kept_ref[...], arrived_ref[...], near, [rows for _, rows in loaded], passed, capacity
    )
    features_out[...] = (local_ref[...] + dot(onehot_ref[...], returned.astype(BF16), TN)).astype(BF16)
    total = own_ref[...] + near_tile + passed_tile + sum(tiles[:tall] for tiles, _ in loaded)
    weight_out[...] = total * (1.0 / math.sqrt(devices))


def body(features, neighbours, send_rows, send_counts, candidates, perturbation, weight):
    towers = lax.axis_size("z")
    replicas = lax.axis_size("replica")
    groups = 2 * towers
    devices = groups * replicas
    capacity = send_rows.shape[3]
    _, rows, width = features.shape
    _, queries, samples, cands = perturbation.shape
    fanout = neighbours.shape[2]
    slots = groups * capacity
    parts = width // LANES
    passes = towers // 2 - 1
    noise_rows = queries * samples * (cands // LANES)
    noise = (
        perturbation.reshape(queries, samples, cands // LANES, LANES)
        .transpose(0, 2, 1, 3)
        .reshape(noise_rows, LANES)
    )
    hbm = pl.BlockSpec(memory_space=pltpu.HBM)
    vmem = pl.BlockSpec(memory_space=pltpu.VMEM)
    shape = jax.ShapeDtypeStruct

    def call(kernel, name, operands, out_shape, from_hbm=(), scratch=()):
        from_hbm = [pltpu.with_memory_space_constraint(x, pltpu.HBM) for x in from_hbm]
        return pl.pallas_call(
            kernel,
            out_shape=out_shape,
            in_specs=[hbm] * len(from_hbm) + [vmem] * len(operands),
            out_specs=jax.tree.map(lambda _: vmem, out_shape),
            scratch_shapes=scratch,
            compiler_params=pltpu.CompilerParams(vmem_limit_bytes=32 * 1024 * 1024),
            name=name,
        )(*from_hbm, *operands)

    def swap_core(array):
        return lax.ppermute(array, "core", [(0, 1), (1, 0)])

    def swap_near(array):
        return lax.ppermute(array, "z", [(i, i ^ towers // 2) for i in range(towers)])

    def swap_far(arrays):
        return [
            lax.ppermute(
                array,
                ("z", "core"),
                [(2 * i + c, 2 * (i ^ j + c * towers // 2) + c) for i in range(towers) for c in range(2)],
            )
            for j, array in enumerate(arrays, 1)
        ]

    def swap_replica(arrays):
        return [
            lax.ppermute(array, "replica", [(i, i ^ s) for i in range(replicas)])
            for array, s in zip(arrays, range(replicas - 1, 0, -1))
        ]

    half = shape((slots // 2, width), F32)
    kept, sent, onehot, held, feature_rows, neighbour_rows = call(
        functools.partial(outgoing_kernel, towers, capacity),
        "outgoing",
        [],
        [
            half,
            half,
            shape((slots, rows), BF16),
            shape((slots, rows), F32),
            shape((rows, width), BF16),
            shape((fanout, rows), jnp.int32),
        ],
        [
            jnp.swapaxes(send_rows[0, 0], 0, 1),
            send_counts[0],
            features[0],
            jnp.swapaxes(neighbours[0], 0, 1),
        ],
        (
            pltpu.SMEM((capacity, groups), jnp.int32),
            pltpu.SMEM((1, groups), jnp.int32),
            pltpu.SemaphoreType.DMA((4,)),
        ),
    )
    arrived = swap_core(sent)
    own, far, far_turned, start = call(
        functools.partial(adjacency_kernel, towers, capacity),
        "adjacency",
        [held, feature_rows, neighbour_rows],
        [
            shape((rows, rows), BF16),
            shape((slots, rows), BF16),
            shape((rows, slots), BF16),
            shape((rows, width), F32),
        ],
    )
    near, *far_sent = call(
        functools.partial(hop_kernel, capacity),
        "halo_hop",
        [far, kept, arrived],
        [shape((2 * capacity, width), BF16)] + [shape((4 * capacity, width), BF16)] * passes,
    )
    far_halo = swap_far(far_sent)
    near = swap_near(near)
    passed = swap_core(
        call(
            functools.partial(pass_kernel, capacity),
            "halo_pass",
            far_halo,
            shape((2 * capacity * passes, width), BF16),
        )
    )
    candidate_rows, noise, weight, marks = call(
        prepare_kernel,
        "prepare",
        [],
        [
            shape((queries, cands), jnp.int32),
            shape((noise_rows, LANES), F32),
            shape((width, width), BF16),
            shape((DIGIT * queries, cands), BF16),
        ],
        [candidates[0], noise, weight],
        (pltpu.VMEM((noise_rows, LANES), F32), pltpu.SemaphoreType.DMA((3,))),
    )
    kept_turned, sent, d_pre = call(
        functools.partial(main_kernel, towers, capacity, fanout),
        "forward_backward",
        [far_turned, start, candidate_rows, noise, weight, marks, kept, arrived, *far_halo, passed, near],
        [
            shape((width // 2, rows), BF16),
            shape((width // 2, width), BF16),
            shape((rows, width), BF16),
        ],
    )

    arrived = swap_core(sent)
    kept = call(own_term_kernel, "own_term", [kept_turned, d_pre], shape((width // 2, width), F32))
    local, halo_kept, halo_sent = call(
        functools.partial(spread_kernel, towers, capacity, fanout),
        "spread",
        [d_pre, weight, own, far],
        [shape((rows, width), F32), half, half],
    )
    halo_arrived = swap_core(halo_sent)
    tall, wide = width // groups, width // replicas
    own_term, *terms = call(
        functools.partial(core_sum_kernel, replicas),
        "core_sum",
        [kept, arrived],
        [shape((width // 2, wide), F32)] + [shape((width // 2, wide), BF16)] * (replicas - 1),
    )
    terms = swap_replica(terms)

    def block(tiles, slot_count, dtype):
        return shape((-(-tiles * tall // 16) * 16 + slot_count * capacity * parts, LANES), dtype)

    own_tile, near, *far_sent = call(
        functools.partial(replica_sum_kernel, replicas, capacity),
        "replica_sum",
        [own_term, *terms, halo_kept, halo_arrived],
        [shape((tall, wide), F32), block(1, 2, BF16)] + [block(2, 4, BF16)] * passes,
    )
    far_sums = swap_far(far_sent)
    near = swap_near(near)
    passed = swap_core(
        call(
            functools.partial(pass_sums_kernel, capacity, parts, tall, wide),
            "pass_sums",
            far_sums,
            block(1, 2 * passes, BF16),
        )
    )
    d_features, weight_grad = call(
        functools.partial(final_kernel, capacity, devices),
        "final",
        [local, onehot, halo_kept, halo_arrived, own_tile, *far_sums, passed, near],
        [shape((rows, width), BF16), shape((tall, wide), F32)],
    )
    return (d_features[None], weight_grad)


def solution(mesh):
    groups, replicas = mesh.devices.shape
    split = jax.sharding.Mesh(
        mesh.devices.reshape(groups // 2, 2, replicas), ("z", "core", "replica")
    )
    graph = ("z", "core")
    placed = (
        P("replica", graph, None),
        P("replica", graph, None),
        P("replica", graph, None, None),
        P("replica", graph, None),
        P("replica", graph, None),
        P("replica", graph, None, None),
        P(),
    )
    return jax.shard_map(
        body,
        mesh=split,
        in_specs=placed,
        out_specs=(P("replica", graph, None), P(graph, "replica")),
        check_vma=False,
    )
```

```python
import functools
import math

import jax
import jax.numpy as jnp
from jax import lax
from jax.experimental import pallas as pl
from jax.experimental.pallas import tpu as pltpu
from jax.sharding import PartitionSpec as P

TOP = 20
SCORE_SCALE = 16.0
LOSS_SCALE = 16.0
EPSILON = 1e-05
LANES = 128
DIGIT = 16
F32 = jnp.float32
BF16 = jnp.bfloat16
NN = (((1,), (0,)), ((), ()))
TN = (((0,), (0,)), ((), ()))
NT = (((1,), (1,)), ((), ()))


def dot(a, b, dims):
    return lax.dot_general(a, b, dims, preferred_element_type=F32)


def slot_device(slot, towers):
    core = lax.axis_index("core")
    pair, e = slot // 2, slot % 2
    mixed = jnp.where(pair > 1, 1, 0)
    odd = pair % 2 * mixed
    upper = pair % 2 * (1 - mixed) + lax.bitwise_xor(core, odd) * mixed
    z = lax.bitwise_xor(lax.axis_index("z"), pair // 2 + upper * (towers // 2))
    return 2 * z + lax.bitwise_xor(core, lax.bitwise_xor(odd, jnp.int32(e)))


def kept_slots(towers):
    return [0, 2] + [4 * j + e for j in range(1, towers // 2) for e in range(2)]


def sent_slots(towers):
    return [1, 3] + [4 * j + 2 + e for j in range(1, towers // 2) for e in range(2)]


def slot_tiles(tiles):
    core = lax.axis_index("core")
    pairs = [xor_order(tiles[2 * z : 2 * z + 2], core) for z in range(len(tiles) // 2)]
    same = xor_order([pair[0] for pair in pairs], lax.axis_index("z"))
    other = xor_order([pair[1] for pair in pairs], lax.axis_index("z"))
    half = len(pairs) // 2
    ordered = [same[0], other[0], same[half], other[half]]
    for j in range(1, half):
        first = [xor_order([found[j], found[half + j]], core) for found in (same, other)]
        ordered += [first[0][0], first[1][0], first[1][1], first[0][1]]
    return ordered


def pick(array, slots, size):
    return jnp.concatenate([array[i * size : (i + 1) * size] for i in slots], axis=0)


def fold(rows):
    return jnp.concatenate(
        [rows[:, j : j + LANES] for j in range(0, rows.shape[1], LANES)], axis=0
    )


def unfold(block, parts):
    size = block.shape[0] // parts
    return jnp.concatenate([block[j * size : (j + 1) * size] for j in range(parts)], axis=1)


def near_rows(kept, arrived, size):
    return jnp.concatenate([pick(kept, [1], size), pick(arrived, [1], size)], axis=0)


def far_rows(kept, arrived, j, size):
    return jnp.concatenate([pick(x, [2 * j, 2 * j + 1], size) for x in (kept, arrived)], axis=0)


def slot_rows(kept, arrived, near, far, passed, size):
    rows = [pick(kept, [0], size), pick(arrived, [0], size), near]
    for j, block in enumerate(far):
        rows += [pick(block, [0, 2], size), pick(passed, [2 * j, 2 * j + 1], size)]
    return jnp.concatenate(rows, axis=0)


def xor_order(pieces, me):
    bit = 1
    while bit < len(pieces):
        swap = lax.bitwise_and(me, jnp.int32(bit)) != 0
        pieces = [jnp.where(swap, pieces[i ^ bit], pieces[i]) for i in range(len(pieces))]
        bit *= 2
    return pieces


def start_copies(pairs, sems):
    copies = [pltpu.make_async_copy(a, b, sems.at[i]) for i, (a, b) in enumerate(pairs)]
    for copy in copies:
        copy.start()
    return copies


def outgoing_kernel(
    towers,
    capacity,
    send_hbm,
    counts_hbm,
    features_hbm,
    neighbours_hbm,
    candidates_hbm,
    noise_hbm,
    kept_ref,
    sent_ref,
    onehot_ref,
    held_ref,
    features_ref,
    neighbours_ref,
    candidates_ref,
    noise_ref,
    send_smem,
    counts_smem,
    sems,
):
    copies = start_copies(
        [
            (send_hbm, send_smem),
            (counts_hbm, counts_smem),
            (features_hbm, features_ref),
            (neighbours_hbm, neighbours_ref),
            (candidates_hbm, candidates_ref),
            (noise_hbm, noise_ref),
        ],
        sems,
    )
    rows = features_ref.shape[0]
    slots = 2 * towers * capacity
    slot = lax.broadcasted_iota(jnp.int32, (slots, rows), 0)
    row = lax.broadcasted_iota(jnp.int32, (slots, rows), 1)
    named = jnp.full((slots, rows), -1, jnp.int32)
    held = jnp.zeros((slots, rows), jnp.int32)
    copies[0].wait()
    copies[1].wait()
    for i in range(2 * towers):
        device = slot_device(i, towers)
        held = jnp.where(slot // capacity == i, counts_smem[0, device], held)
        for k in range(capacity):
            named = jnp.where(slot == i * capacity + k, send_smem[k, device], named)
    onehot = (named == row).astype(F32).astype(BF16)
    onehot_ref[...] = onehot
    held_ref[...] = (slot % capacity < held).astype(F32)
    copies[2].wait()
    picked = dot(onehot, features_ref[...], NN)
    kept_ref[...] = pick(picked, kept_slots(towers), capacity)
    sent_ref[...] = pick(picked, sent_slots(towers), capacity)
    for copy in copies[3:]:
        copy.wait()


def hop_kernel(capacity, after_ref, kept_ref, arrived_ref, near_ref, *far_refs):
    kept, arrived = kept_ref[...], arrived_ref[...]
    near_ref[...] = near_rows(kept, arrived, capacity).astype(BF16)
    for j, ref in enumerate(far_refs):
        ref[...] = far_rows(kept, arrived, j + 1, capacity).astype(BF16)


def pass_kernel(capacity, *refs):
    far_refs, out_ref = refs[:-1], refs[-1]
    rows = [pick(ref[...].astype(F32), [1, 3], capacity) for ref in far_refs]
    out_ref[...] = jnp.concatenate(rows, axis=0).astype(BF16)


def prepare_kernel(
    towers,
    capacity,
    held_ref,
    features_ref,
    neighbours_ref,
    candidates_ref,
    raw_noise_ref,
    own_ref,
    far_ref,
    far_turned_ref,
    start_ref,
    marks_ref,
    noise_ref,
):
    rows = features_ref.shape[0]
    fanout = neighbours_ref.shape[0]
    slots = far_ref.shape[0]
    own = lax.broadcasted_iota(jnp.int32, (rows, rows), 0)
    far = lax.broadcasted_iota(jnp.int32, (slots, rows), 0)
    far_slot = slot_device(far // capacity, towers) * capacity + far % capacity + rows
    own_count = jnp.zeros((rows, rows), F32)
    far_count = jnp.zeros((slots, rows), F32)
    for f in range(fanout):
        named = neighbours_ref[f : f + 1, :]
        own_count = own_count + (own == named).astype(F32)
        far_count = far_count + (far_slot == named).astype(F32)
    own_count = own_count.astype(BF16)
    far_count = far_count * held_ref[...]
    far_ref[...] = far_count.astype(BF16)
    far_turned_ref[...] = far_count.T.astype(BF16)
    own_ref[...] = own_count
    features = features_ref[...]
    start_ref[...] = features.astype(F32) + dot(own_count, features, TN)
    queries, cands = candidates_ref.shape
    blocks = cands // LANES
    samples = noise_ref.shape[0] // (queries * blocks)
    low = lax.bitwise_and(candidates_ref[...], jnp.int32(DIGIT - 1))
    for digit in range(DIGIT):
        marks_ref[digit * queries : (digit + 1) * queries, :] = (
            (low == digit).astype(F32).astype(BF16)
        )
    for m in range(samples):
        noise = [
            raw_noise_ref[pl.ds(j * samples + m, queries, stride=blocks * samples), :]
            for j in range(blocks)
        ]
        highest = jnp.max(functools.reduce(jnp.maximum, noise), axis=-1, keepdims=True)
        for j in range(blocks):
            at = (m * blocks + j) * queries
            noise_ref[at : at + queries, :] = jnp.exp(noise[j] - highest)


def weight_kernel(weight_hbm, weight_ref, sem):
    copy = pltpu.make_async_copy(weight_hbm, weight_ref, sem)
    copy.start()
    copy.wait()


def main_kernel(
    towers,
    capacity,
    fanout,
    far_turned_ref,
    start_ref,
    candidates_ref,
    noise_ref,
    weight_ref,
    marks_ref,
    halo_kept_ref,
    halo_arrived_ref,
    *refs,
):
    *halo_refs, kept_turned_ref, sent_ref, d_pre_ref = refs
    *far_halo, passed, near = [ref[...].astype(F32) for ref in halo_refs]
    rows, width = start_ref.shape
    queries, cands = candidates_ref.shape
    samples = noise_ref.shape[0] // (queries * (cands // LANES))
    halo = slot_rows(halo_kept_ref[...], halo_arrived_ref[...], near, far_halo, passed, capacity)
    sums = start_ref[...] + dot(far_turned_ref[...], halo.astype(BF16), NN)
    mean_rows = (sums * (1.0 / (fanout + 1))).astype(BF16)

    tall = width // (2 * towers)
    turned = mean_rows.astype(F32).T
    tiles = slot_tiles([turned[i * tall : (i + 1) * tall] for i in range(2 * towers)])
    kept_turned, sent_turned = [
        jnp.concatenate([tiles[i] for i in slots], axis=0).astype(BF16)
        for slots in (kept_slots(towers), sent_slots(towers))
    ]

    weight = weight_ref[...]
    pre = dot(mean_rows, weight, NN)
    inverse = lax.rsqrt(jnp.mean(pre * pre, axis=-1, keepdims=True) + EPSILON)
    embedded = (pre * inverse).astype(BF16)
    factor = SCORE_SCALE / width
    rounded = pre.astype(BF16)
    similar = dot(rounded[:queries], rounded, NT)
    inverse_of_column = jnp.broadcast_to(inverse, (rows, rows)).T[:queries]
    similar = similar * (factor * inverse[:queries] * inverse_of_column)
    blocks = cands // LANES
    scores = [
        jnp.take_along_axis(similar, candidates_ref[:, j * LANES : (j + 1) * LANES], axis=1)
        for j in range(blocks)
    ]
    grown = [jnp.exp(x) for x in scores]
    soft = [jnp.zeros((queries, LANES), F32) for _ in range(blocks)]
    for m in range(samples):
        at = m * blocks * queries
        noise = [noise_ref[at + j * queries : at + (j + 1) * queries, :] for j in range(blocks)]
        total = jnp.sum(sum(n * g for n, g in zip(noise, grown)), axis=-1, keepdims=True)
        scale = (LOSS_SCALE * TOP / samples) / total
        soft = [a + n * scale for a, n in zip(soft, noise)]
    soft = [a * g for a, g in zip(soft, grown)]
    lane = lax.broadcasted_iota(jnp.int32, (queries, LANES), 1)
    d_scores = [
        jnp.where(lane + j * LANES < TOP, s - LOSS_SCALE, s) if j * LANES < TOP else s
        for j, s in enumerate(soft)
    ]
    d_scores = jnp.concatenate(d_scores, axis=1)

    high = candidates_ref[...] // DIGIT
    digits = rows // DIGIT
    weighted = [jnp.where(high == digit, d_scores, 0.0) for digit in range(digits)]
    crossed = dot(marks_ref[...], jnp.concatenate(weighted, axis=0).astype(BF16), NT)
    q_row = lax.broadcasted_iota(jnp.int32, crossed.shape, 0) % queries
    q_column = lax.broadcasted_iota(jnp.int32, crossed.shape, 1) % queries
    crossed = jnp.where(q_row == q_column, crossed, 0.0)
    kept = jnp.sum(crossed.reshape(DIGIT, queries, digits * queries), axis=1)
    d_similar = jnp.concatenate(
        [kept[:, i * queries : (i + 1) * queries] for i in range(digits)], axis=0
    ).astype(BF16)

    d_embedded = factor * dot(d_similar, embedded[:queries], NN)
    d_queries = factor * dot(d_similar, embedded, TN)
    d_embedded = jnp.concatenate(
        [d_embedded[:queries] + d_queries, d_embedded[queries:]], axis=0
    )
    inner = jnp.mean(d_embedded * pre, axis=-1, keepdims=True)
    d_pre = (inverse * d_embedded - inverse * inverse * inverse * pre * inner).astype(BF16)

    d_pre_ref[...] = d_pre
    sent_ref[...] = dot(sent_turned, d_pre, NN).astype(BF16)
    kept_turned_ref[...] = kept_turned


def own_term_kernel(kept_turned_ref, d_pre_ref, out_ref):
    out_ref[...] = dot(kept_turned_ref[...], d_pre_ref[...], NN)


def spread_kernel(
    towers, capacity, fanout, d_pre_ref, weight_ref, own_ref, far_ref, local_ref, kept_ref, sent_ref
):
    share = (dot(d_pre_ref[...], weight_ref[...], NT) * (1.0 / (fanout + 1))).astype(BF16)
    halo_grad = dot(far_ref[...], share, NN)
    kept_ref[...] = pick(halo_grad, kept_slots(towers), capacity)
    sent_ref[...] = pick(halo_grad, sent_slots(towers), capacity)
    local_ref[...] = share.astype(F32) + dot(own_ref[...], share, NN)


def core_sum_kernel(replicas, kept_ref, arrived_ref, own_ref, *out_refs):
    total = kept_ref[...] + arrived_ref[...].astype(F32)
    wide = total.shape[1] // replicas
    pieces = [total[:, r * wide : (r + 1) * wide] for r in range(replicas)]
    pieces = xor_order(pieces, lax.axis_index("replica"))
    own_ref[...] = pieces[0]
    for ref, piece in zip(out_refs, pieces[:0:-1]):
        ref[...] = piece.astype(BF16)


def store_block(ref, tiles, rows):
    high, wide = tiles.shape
    block = fold(rows)
    if (high + block.shape[0], wide) != ref.shape:
        ref[...] = jnp.zeros(ref.shape, ref.dtype)
    ref[0:high, 0:wide] = tiles.astype(ref.dtype)
    ref[ref.shape[0] - block.shape[0] :, :] = block.astype(ref.dtype)


def load_block(ref, high, wide, slots, parts):
    block = ref[...].astype(F32)
    return block[:high, :wide], unfold(block[block.shape[0] - slots * parts :], parts)


def replica_sum_kernel(replicas, capacity, *refs):
    term_refs, refs = refs[:replicas], refs[replicas:]
    kept_ref, arrived_ref, own_ref, near_ref, *far_refs = refs
    total = sum(ref[...].astype(F32) for ref in term_refs)
    tall = own_ref.shape[0]
    kept, arrived = kept_ref[...], arrived_ref[...]
    own_ref[...] = total[:tall]
    store_block(near_ref, total[tall : 2 * tall], near_rows(kept, arrived, capacity))
    for j, ref in enumerate(far_refs):
        tiles = total[2 * (j + 1) * tall : 2 * (j + 2) * tall]
        store_block(ref, tiles, far_rows(kept, arrived, j + 1, capacity))


def pass_sums_kernel(capacity, parts, tall, wide, *refs):
    far_refs, out_ref = refs[:-1], refs[-1]
    loaded = [load_block(ref, 2 * tall, wide, 4 * capacity, parts) for ref in far_refs]
    store_block(
        out_ref,
        sum(tiles[tall:] for tiles, _ in loaded),
        jnp.concatenate([pick(rows, [1, 3], capacity) for _, rows in loaded], axis=0),
    )


def final_kernel(capacity, devices, local_ref, onehot_ref, kept_ref, arrived_ref, own_ref, *refs):
    *far_refs, passed_ref, near_ref, features_out, weight_out = refs
    tall, wide = own_ref.shape
    parts = local_ref.shape[1] // LANES
    near_tile, near = load_block(near_ref, tall, wide, 2 * capacity, parts)
    loaded = [load_block(ref, 2 * tall, wide, 4 * capacity, parts) for ref in far_refs]
    passed_tile, passed = load_block(passed_ref, tall, wide, 2 * capacity * len(far_refs), parts)
    returned = slot_rows(
        kept_ref[...], arrived_ref[...], near, [rows for _, rows in loaded], passed, capacity
    )
    features_out[...] = (local_ref[...] + dot(onehot_ref[...], returned.astype(BF16), TN)).astype(BF16)
    total = own_ref[...] + near_tile + passed_tile + sum(tiles[:tall] for tiles, _ in loaded)
    weight_out[...] = total * (1.0 / math.sqrt(devices))


def body(features, neighbours, send_rows, send_counts, candidates, perturbation, weight):
    towers = lax.axis_size("z")
    replicas = lax.axis_size("replica")
    groups = 2 * towers
    devices = groups * replicas
    capacity = send_rows.shape[3]
    _, rows, width = features.shape
    _, queries, samples, cands = perturbation.shape
    fanout = neighbours.shape[2]
    slots = groups * capacity
    parts = width // LANES
    passes = towers // 2 - 1
    noise_rows = queries * samples * (cands // LANES)
    noise = (
        perturbation.reshape(queries, samples, cands // LANES, LANES)
        .transpose(0, 2, 1, 3)
        .reshape(noise_rows, LANES)
    )
    hbm = pl.BlockSpec(memory_space=pltpu.HBM)
    vmem = pl.BlockSpec(memory_space=pltpu.VMEM)
    shape = jax.ShapeDtypeStruct

    def call(kernel, name, operands, out_shape, from_hbm=(), scratch=()):
        from_hbm = [pltpu.with_memory_space_constraint(x, pltpu.HBM) for x in from_hbm]
        return pl.pallas_call(
            kernel,
            out_shape=out_shape,
            in_specs=[hbm] * len(from_hbm) + [vmem] * len(operands),
            out_specs=jax.tree.map(lambda _: vmem, out_shape),
            scratch_shapes=scratch,
            compiler_params=pltpu.CompilerParams(vmem_limit_bytes=32 * 1024 * 1024),
            name=name,
        )(*from_hbm, *operands)

    def swap_core(array):
        return lax.ppermute(array, "core", [(0, 1), (1, 0)])

    def swap_near(array):
        return lax.ppermute(array, "z", [(i, i ^ towers // 2) for i in range(towers)])

    def swap_far(arrays):
        return [
            lax.ppermute(
                array,
                ("z", "core"),
                [(2 * i + c, 2 * (i ^ j + c * towers // 2) + c) for i in range(towers) for c in range(2)],
            )
            for j, array in enumerate(arrays, 1)
        ]

    def swap_replica(arrays):
        return [
            lax.ppermute(array, "replica", [(i, i ^ s) for i in range(replicas)])
            for array, s in zip(arrays, range(replicas - 1, 0, -1))
        ]

    half = shape((slots // 2, width), F32)
    kept, sent, onehot, held, feature_rows, neighbour_rows, candidate_rows, noise = call(
        functools.partial(outgoing_kernel, towers, capacity),
        "outgoing",
        [],
        [
            half,
            half,
            shape((slots, rows), BF16),
            shape((slots, rows), F32),
            shape((rows, width), BF16),
            shape((fanout, rows), jnp.int32),
            shape((queries, cands), jnp.int32),
            shape((noise_rows, LANES), F32),
        ],
        [
            jnp.swapaxes(send_rows[0, 0], 0, 1),
            send_counts[0],
            features[0],
            jnp.swapaxes(neighbours[0], 0, 1),
            candidates[0],
            noise,
        ],
        (
            pltpu.SMEM((capacity, groups), jnp.int32),
            pltpu.SMEM((1, groups), jnp.int32),
            pltpu.SemaphoreType.DMA((6,)),
        ),
    )
    arrived = swap_core(sent)
    own, far, far_turned, start, marks, noise = call(
        functools.partial(prepare_kernel, towers, capacity),
        "prepare",
        [held, feature_rows, neighbour_rows, candidate_rows, noise],
        [
            shape((rows, rows), BF16),
            shape((slots, rows), BF16),
            shape((rows, slots), BF16),
            shape((rows, width), F32),
            shape((DIGIT * queries, cands), BF16),
            shape((noise_rows, LANES), F32),
        ],
    )
    near, *far_sent = call(
        functools.partial(hop_kernel, capacity),
        "halo_hop",
        [far, kept, arrived],
        [shape((2 * capacity, width), BF16)] + [shape((4 * capacity, width), BF16)] * passes,
    )
    far_halo = swap_far(far_sent)
    near = swap_near(near)
    passed = swap_core(
        call(
            functools.partial(pass_kernel, capacity),
            "halo_pass",
            far_halo,
            shape((2 * capacity * passes, width), BF16),
        )
    )
    weight = call(
        weight_kernel,
        "weight",
        [],
        shape((width, width), BF16),
        [weight],
        (pltpu.SemaphoreType.DMA,),
    )
    kept_turned, sent, d_pre = call(
        functools.partial(main_kernel, towers, capacity, fanout),
        "forward_backward",
        [far_turned, start, candidate_rows, noise, weight, marks, kept, arrived, *far_halo, passed, near],
        [
            shape((width // 2, rows), BF16),
            shape((width // 2, width), BF16),
            shape((rows, width), BF16),
        ],
    )

    arrived = swap_core(sent)
    kept = call(own_term_kernel, "own_term", [kept_turned, d_pre], shape((width // 2, width), F32))
    local, halo_kept, halo_sent = call(
        functools.partial(spread_kernel, towers, capacity, fanout),
        "spread",
        [d_pre, weight, own, far],
        [shape((rows, width), F32), half, half],
    )
    halo_arrived = swap_core(halo_sent)
    tall, wide = width // groups, width // replicas
    own_term, *terms = call(
        functools.partial(core_sum_kernel, replicas),
        "core_sum",
        [kept, arrived],
        [shape((width // 2, wide), F32)] + [shape((width // 2, wide), BF16)] * (replicas - 1),
    )
    terms = swap_replica(terms)

    def block(tiles, slot_count, dtype):
        return shape((-(-tiles * tall // 16) * 16 + slot_count * capacity * parts, LANES), dtype)

    own_tile, near, *far_sent = call(
        functools.partial(replica_sum_kernel, replicas, capacity),
        "replica_sum",
        [own_term, *terms, halo_kept, halo_arrived],
        [shape((tall, wide), F32), block(1, 2, BF16)] + [block(2, 4, BF16)] * passes,
    )
    far_sums = swap_far(far_sent)
    near = swap_near(near)
    passed = swap_core(
        call(
            functools.partial(pass_sums_kernel, capacity, parts, tall, wide),
            "pass_sums",
            far_sums,
            block(1, 2 * passes, BF16),
        )
    )
    d_features, weight_grad = call(
        functools.partial(final_kernel, capacity, devices),
        "final",
        [local, onehot, halo_kept, halo_arrived, own_tile, *far_sums, passed, near],
        [shape((rows, width), BF16), shape((tall, wide), F32)],
    )
    return (d_features[None], weight_grad)


def solution(mesh):
    groups, replicas = mesh.devices.shape
    split = jax.sharding.Mesh(
        mesh.devices.reshape(groups // 2, 2, replicas), ("z", "core", "replica")
    )
    graph = ("z", "core")
    placed = (
        P("replica", graph, None),
        P("replica", graph, None),
        P("replica", graph, None, None),
        P("replica", graph, None),
        P("replica", graph, None),
        P("replica", graph, None, None),
        P(),
    )
    return jax.shard_map(
        body,
        mesh=split,
        in_specs=placed,
        out_specs=(P("replica", graph, None), P(graph, "replica")),
        check_vma=False,
    )
```

```python
import functools
import math

import jax
import jax.numpy as jnp
from jax import lax
from jax.experimental import pallas as pl
from jax.experimental.pallas import tpu as pltpu
from jax.sharding import PartitionSpec as P

TOP = 20
SCORE_SCALE = 16.0
LOSS_SCALE = 16.0
EPSILON = 1e-05
LANES = 128
DIGIT = 16
F32 = jnp.float32
BF16 = jnp.bfloat16
NN = (((1,), (0,)), ((), ()))
TN = (((0,), (0,)), ((), ()))
NT = (((1,), (1,)), ((), ()))


def dot(a, b, dims):
    return lax.dot_general(a, b, dims, preferred_element_type=F32)


def slot_device(slot, towers):
    core = lax.axis_index("core")
    pair, e = slot // 2, slot % 2
    mixed = jnp.where(pair > 1, 1, 0)
    odd = pair % 2 * mixed
    upper = pair % 2 * (1 - mixed) + lax.bitwise_xor(core, odd) * mixed
    z = lax.bitwise_xor(lax.axis_index("z"), pair // 2 + upper * (towers // 2))
    return 2 * z + lax.bitwise_xor(core, lax.bitwise_xor(odd, jnp.int32(e)))


def kept_slots(towers):
    return [0, 2] + [4 * j + e for j in range(1, towers // 2) for e in range(2)]


def sent_slots(towers):
    return [1, 3] + [4 * j + 2 + e for j in range(1, towers // 2) for e in range(2)]


def slot_tiles(tiles):
    core = lax.axis_index("core")
    pairs = [xor_order(tiles[2 * z : 2 * z + 2], core) for z in range(len(tiles) // 2)]
    same = xor_order([pair[0] for pair in pairs], lax.axis_index("z"))
    other = xor_order([pair[1] for pair in pairs], lax.axis_index("z"))
    half = len(pairs) // 2
    ordered = [same[0], other[0], same[half], other[half]]
    for j in range(1, half):
        first = [xor_order([found[j], found[half + j]], core) for found in (same, other)]
        ordered += [first[0][0], first[1][0], first[1][1], first[0][1]]
    return ordered


def pick(array, slots, size):
    return jnp.concatenate([array[i * size : (i + 1) * size] for i in slots], axis=0)


def fold(rows):
    return jnp.concatenate(
        [rows[:, j : j + LANES] for j in range(0, rows.shape[1], LANES)], axis=0
    )


def unfold(block, parts):
    size = block.shape[0] // parts
    return jnp.concatenate([block[j * size : (j + 1) * size] for j in range(parts)], axis=1)


def near_rows(kept, arrived, size):
    return jnp.concatenate([pick(kept, [1], size), pick(arrived, [1], size)], axis=0)


def far_rows(kept, arrived, j, size):
    return jnp.concatenate([pick(x, [2 * j, 2 * j + 1], size) for x in (kept, arrived)], axis=0)


def slot_rows(kept, arrived, near, far, passed, size):
    rows = [pick(kept, [0], size), pick(arrived, [0], size), near]
    for j, block in enumerate(far):
        rows += [pick(block, [0, 2], size), pick(passed, [2 * j, 2 * j + 1], size)]
    return jnp.concatenate(rows, axis=0)


def xor_order(pieces, me):
    bit = 1
    while bit < len(pieces):
        swap = lax.bitwise_and(me, jnp.int32(bit)) != 0
        pieces = [jnp.where(swap, pieces[i ^ bit], pieces[i]) for i in range(len(pieces))]
        bit *= 2
    return pieces


def start_copies(pairs, sems):
    copies = [pltpu.make_async_copy(a, b, sems.at[i]) for i, (a, b) in enumerate(pairs)]
    for copy in copies:
        copy.start()
    return copies


def outgoing_kernel(
    towers,
    capacity,
    send_hbm,
    counts_hbm,
    features_hbm,
    neighbours_hbm,
    kept_ref,
    sent_ref,
    onehot_ref,
    held_ref,
    features_ref,
    neighbours_ref,
    send_smem,
    counts_smem,
    sems,
):
    copies = start_copies(
        [
            (send_hbm, send_smem),
            (counts_hbm, counts_smem),
            (features_hbm, features_ref),
            (neighbours_hbm, neighbours_ref),
        ],
        sems,
    )
    rows = features_ref.shape[0]
    slots = 2 * towers * capacity
    slot = lax.broadcasted_iota(jnp.int32, (slots, rows), 0)
    row = lax.broadcasted_iota(jnp.int32, (slots, rows), 1)
    named = jnp.full((slots, rows), -1, jnp.int32)
    held = jnp.zeros((slots, rows), jnp.int32)
    copies[0].wait()
    copies[1].wait()
    for i in range(2 * towers):
        device = slot_device(i, towers)
        held = jnp.where(slot // capacity == i, counts_smem[0, device], held)
        for k in range(capacity):
            named = jnp.where(slot == i * capacity + k, send_smem[k, device], named)
    onehot = (named == row).astype(F32).astype(BF16)
    onehot_ref[...] = onehot
    held_ref[...] = (slot % capacity < held).astype(F32)
    copies[2].wait()
    picked = dot(onehot, features_ref[...], NN)
    kept_ref[...] = pick(picked, kept_slots(towers), capacity)
    sent_ref[...] = pick(picked, sent_slots(towers), capacity)
    copies[3].wait()


def hop_kernel(capacity, after_ref, kept_ref, arrived_ref, near_ref, *far_refs):
    kept, arrived = kept_ref[...], arrived_ref[...]
    near_ref[...] = near_rows(kept, arrived, capacity).astype(BF16)
    for j, ref in enumerate(far_refs):
        ref[...] = far_rows(kept, arrived, j + 1, capacity).astype(BF16)


def pass_kernel(capacity, *refs):
    far_refs, out_ref = refs[:-1], refs[-1]
    rows = [pick(ref[...].astype(F32), [1, 3], capacity) for ref in far_refs]
    out_ref[...] = jnp.concatenate(rows, axis=0).astype(BF16)


def adjacency_kernel(
    towers,
    capacity,
    held_ref,
    features_ref,
    neighbours_ref,
    own_ref,
    far_ref,
    far_turned_ref,
    start_ref,
):
    rows = features_ref.shape[0]
    fanout = neighbours_ref.shape[0]
    slots = far_ref.shape[0]
    own = lax.broadcasted_iota(jnp.int32, (rows, rows), 0)
    far = lax.broadcasted_iota(jnp.int32, (slots, rows), 0)
    far_slot = slot_device(far // capacity, towers) * capacity + far % capacity + rows
    own_count = jnp.zeros((rows, rows), F32)
    far_count = jnp.zeros((slots, rows), F32)
    for f in range(fanout):
        named = neighbours_ref[f : f + 1, :]
        own_count = own_count + (own == named).astype(F32)
        far_count = far_count + (far_slot == named).astype(F32)
    own_count = own_count.astype(BF16)
    far_count = far_count * held_ref[...]
    far_ref[...] = far_count.astype(BF16)
    far_turned_ref[...] = far_count.T.astype(BF16)
    own_ref[...] = own_count
    features = features_ref[...]
    start_ref[...] = features.astype(F32) + dot(own_count, features, TN)


def prepare_kernel(
    candidates_hbm,
    noise_hbm,
    weight_hbm,
    candidates_ref,
    noise_ref,
    weight_ref,
    marks_ref,
    raw_noise_ref,
    sems,
):
    copies = start_copies(
        [(candidates_hbm, candidates_ref), (noise_hbm, raw_noise_ref), (weight_hbm, weight_ref)], sems
    )
    queries, cands = candidates_ref.shape
    blocks = cands // LANES
    samples = noise_ref.shape[0] // (queries * blocks)
    copies[0].wait()
    low = lax.bitwise_and(candidates_ref[...], jnp.int32(DIGIT - 1))
    for digit in range(DIGIT):
        marks_ref[digit * queries : (digit + 1) * queries, :] = (
            (low == digit).astype(F32).astype(BF16)
        )
    copies[1].wait()
    for m in range(samples):
        noise = [
            raw_noise_ref[pl.ds(j * samples + m, queries, stride=blocks * samples), :]
            for j in range(blocks)
        ]
        highest = jnp.max(functools.reduce(jnp.maximum, noise), axis=-1, keepdims=True)
        for j in range(blocks):
            at = (m * blocks + j) * queries
            noise_ref[at : at + queries, :] = jnp.exp(noise[j] - highest)
    copies[2].wait()


def main_kernel(
    towers,
    capacity,
    fanout,
    far_turned_ref,
    start_ref,
    candidates_ref,
    noise_ref,
    weight_ref,
    marks_ref,
    halo_kept_ref,
    halo_arrived_ref,
    *refs,
):
    *halo_refs, kept_turned_ref, sent_ref, d_pre_ref = refs
    *far_halo, passed, near = [ref[...].astype(F32) for ref in halo_refs]
    rows, width = start_ref.shape
    queries, cands = candidates_ref.shape
    samples = noise_ref.shape[0] // (queries * (cands // LANES))
    halo = slot_rows(halo_kept_ref[...], halo_arrived_ref[...], near, far_halo, passed, capacity)
    sums = start_ref[...] + dot(far_turned_ref[...], halo.astype(BF16), NN)
    mean_rows = (sums * (1.0 / (fanout + 1))).astype(BF16)

    tall = width // (2 * towers)
    turned = mean_rows.astype(F32).T
    tiles = slot_tiles([turned[i * tall : (i + 1) * tall] for i in range(2 * towers)])
    kept_turned, sent_turned = [
        jnp.concatenate([tiles[i] for i in slots], axis=0).astype(BF16)
        for slots in (kept_slots(towers), sent_slots(towers))
    ]

    weight = weight_ref[...]
    pre = dot(mean_rows, weight, NN)
    inverse = lax.rsqrt(jnp.mean(pre * pre, axis=-1, keepdims=True) + EPSILON)
    embedded = (pre * inverse).astype(BF16)
    factor = SCORE_SCALE / width
    rounded = pre.astype(BF16)
    products = dot(rounded[:queries], rounded, NT)
    turned_products = dot(rounded, rounded[:queries], NT)
    inverse_of_column = jnp.broadcast_to(inverse, (rows, rows)).T
    similar = products * (factor * inverse[:queries] * inverse_of_column[:queries])
    blocks = cands // LANES
    scores = [
        jnp.take_along_axis(similar, candidates_ref[:, j * LANES : (j + 1) * LANES], axis=1)
        for j in range(blocks)
    ]
    grown = [jnp.exp(x) for x in scores]
    soft = [jnp.zeros((queries, LANES), F32) for _ in range(blocks)]
    for m in range(samples):
        at = m * blocks * queries
        noise = [noise_ref[at + j * queries : at + (j + 1) * queries, :] for j in range(blocks)]
        total = jnp.sum(sum(n * g for n, g in zip(noise, grown)), axis=-1, keepdims=True)
        scale = (LOSS_SCALE * TOP / samples) / total
        soft = [a + n * scale for a, n in zip(soft, noise)]
    soft = [a * g for a, g in zip(soft, grown)]
    lane = lax.broadcasted_iota(jnp.int32, (queries, LANES), 1)
    d_scores = [
        jnp.where(lane + j * LANES < TOP, s - LOSS_SCALE, s) if j * LANES < TOP else s
        for j, s in enumerate(soft)
    ]
    d_scores = jnp.concatenate(d_scores, axis=1)

    high = candidates_ref[...] // DIGIT
    digits = rows // DIGIT
    weighted = [jnp.where(high == digit, d_scores, 0.0) for digit in range(digits)]
    crossed = dot(marks_ref[...], jnp.concatenate(weighted, axis=0).astype(BF16), NT)
    q_row = lax.broadcasted_iota(jnp.int32, crossed.shape, 0) % queries
    q_column = lax.broadcasted_iota(jnp.int32, crossed.shape, 1) % queries
    crossed = jnp.where(q_row == q_column, crossed, 0.0)
    kept = jnp.sum(crossed.reshape(DIGIT, queries, digits * queries), axis=1)
    d_similar = jnp.concatenate(
        [kept[:, i * queries : (i + 1) * queries] for i in range(digits)], axis=0
    ).astype(BF16)

    d_embedded = factor * dot(d_similar, embedded[:queries], NN)
    d_queries = factor * dot(d_similar, embedded, TN)
    d_embedded = jnp.concatenate(
        [d_embedded[:queries] + d_queries, d_embedded[queries:]], axis=0
    )
    wide = d_similar.astype(F32)
    inner = jnp.sum(wide * turned_products * inverse_of_column[:, :queries], axis=-1, keepdims=True)
    inner_queries = jnp.sum(wide.T * products * inverse_of_column[:queries], axis=-1, keepdims=True)
    inner = (factor / width) * jnp.concatenate(
        [inner[:queries] + inner_queries, inner[queries:]], axis=0
    )
    d_pre = (inverse * d_embedded - inverse * inverse * inverse * pre * inner).astype(BF16)

    d_pre_ref[...] = d_pre
    sent_ref[...] = dot(sent_turned, d_pre, NN).astype(BF16)
    kept_turned_ref[...] = kept_turned


def own_term_kernel(kept_turned_ref, d_pre_ref, out_ref):
    out_ref[...] = dot(kept_turned_ref[...], d_pre_ref[...], NN)


def spread_kernel(
    towers, capacity, fanout, d_pre_ref, weight_ref, own_ref, far_ref, local_ref, kept_ref, sent_ref
):
    share = (dot(d_pre_ref[...], weight_ref[...], NT) * (1.0 / (fanout + 1))).astype(BF16)
    halo_grad = dot(far_ref[...], share, NN)
    kept_ref[...] = pick(halo_grad, kept_slots(towers), capacity)
    sent_ref[...] = pick(halo_grad, sent_slots(towers), capacity)
    local_ref[...] = share.astype(F32) + dot(own_ref[...], share, NN)


def core_sum_kernel(replicas, kept_ref, arrived_ref, own_ref, *out_refs):
    total = kept_ref[...] + arrived_ref[...].astype(F32)
    wide = total.shape[1] // replicas
    pieces = [total[:, r * wide : (r + 1) * wide] for r in range(replicas)]
    pieces = xor_order(pieces, lax.axis_index("replica"))
    own_ref[...] = pieces[0]
    for ref, piece in zip(out_refs, pieces[:0:-1]):
        ref[...] = piece.astype(BF16)


def store_block(ref, tiles, rows):
    high, wide = tiles.shape
    block = fold(rows)
    if (high + block.shape[0], wide) != ref.shape:
        ref[...] = jnp.zeros(ref.shape, ref.dtype)
    ref[0:high, 0:wide] = tiles.astype(ref.dtype)
    ref[ref.shape[0] - block.shape[0] :, :] = block.astype(ref.dtype)


def load_block(ref, high, wide, slots, parts):
    block = ref[...].astype(F32)
    return block[:high, :wide], unfold(block[block.shape[0] - slots * parts :], parts)


def replica_sum_kernel(replicas, capacity, *refs):
    term_refs, refs = refs[:replicas], refs[replicas:]
    kept_ref, arrived_ref, own_ref, near_ref, *far_refs = refs
    total = sum(ref[...].astype(F32) for ref in term_refs)
    tall = own_ref.shape[0]
    kept, arrived = kept_ref[...], arrived_ref[...]
    own_ref[...] = total[:tall]
    store_block(near_ref, total[tall : 2 * tall], near_rows(kept, arrived, capacity))
    for j, ref in enumerate(far_refs):
        tiles = total[2 * (j + 1) * tall : 2 * (j + 2) * tall]
        store_block(ref, tiles, far_rows(kept, arrived, j + 1, capacity))


def pass_sums_kernel(capacity, parts, tall, wide, *refs):
    far_refs, out_ref = refs[:-1], refs[-1]
    loaded = [load_block(ref, 2 * tall, wide, 4 * capacity, parts) for ref in far_refs]
    store_block(
        out_ref,
        sum(tiles[tall:] for tiles, _ in loaded),
        jnp.concatenate([pick(rows, [1, 3], capacity) for _, rows in loaded], axis=0),
    )


def final_kernel(capacity, devices, local_ref, onehot_ref, kept_ref, arrived_ref, own_ref, *refs):
    *far_refs, passed_ref, near_ref, features_out, weight_out = refs
    tall, wide = own_ref.shape
    parts = local_ref.shape[1] // LANES
    near_tile, near = load_block(near_ref, tall, wide, 2 * capacity, parts)
    loaded = [load_block(ref, 2 * tall, wide, 4 * capacity, parts) for ref in far_refs]
    passed_tile, passed = load_block(passed_ref, tall, wide, 2 * capacity * len(far_refs), parts)
    returned = slot_rows(
        kept_ref[...], arrived_ref[...], near, [rows for _, rows in loaded], passed, capacity
    )
    features_out[...] = (local_ref[...] + dot(onehot_ref[...], returned.astype(BF16), TN)).astype(BF16)
    total = own_ref[...] + near_tile + passed_tile + sum(tiles[:tall] for tiles, _ in loaded)
    weight_out[...] = total * (1.0 / math.sqrt(devices))


def body(features, neighbours, send_rows, send_counts, candidates, perturbation, weight):
    towers = lax.axis_size("z")
    replicas = lax.axis_size("replica")
    groups = 2 * towers
    devices = groups * replicas
    capacity = send_rows.shape[3]
    _, rows, width = features.shape
    _, queries, samples, cands = perturbation.shape
    fanout = neighbours.shape[2]
    slots = groups * capacity
    parts = width // LANES
    passes = towers // 2 - 1
    noise_rows = queries * samples * (cands // LANES)
    noise = (
        perturbation.reshape(queries, samples, cands // LANES, LANES)
        .transpose(0, 2, 1, 3)
        .reshape(noise_rows, LANES)
    )
    hbm = pl.BlockSpec(memory_space=pltpu.HBM)
    vmem = pl.BlockSpec(memory_space=pltpu.VMEM)
    shape = jax.ShapeDtypeStruct

    def call(kernel, name, operands, out_shape, from_hbm=(), scratch=()):
        from_hbm = [pltpu.with_memory_space_constraint(x, pltpu.HBM) for x in from_hbm]
        return pl.pallas_call(
            kernel,
            out_shape=out_shape,
            in_specs=[hbm] * len(from_hbm) + [vmem] * len(operands),
            out_specs=jax.tree.map(lambda _: vmem, out_shape),
            scratch_shapes=scratch,
            compiler_params=pltpu.CompilerParams(vmem_limit_bytes=32 * 1024 * 1024),
            name=name,
        )(*from_hbm, *operands)

    def swap_core(array):
        return lax.ppermute(array, "core", [(0, 1), (1, 0)])

    def swap_near(array):
        return lax.ppermute(array, "z", [(i, i ^ towers // 2) for i in range(towers)])

    def swap_far(arrays):
        return [
            lax.ppermute(
                array,
                ("z", "core"),
                [(2 * i + c, 2 * (i ^ j + c * towers // 2) + c) for i in range(towers) for c in range(2)],
            )
            for j, array in enumerate(arrays, 1)
        ]

    def swap_replica(arrays):
        return [
            lax.ppermute(array, "replica", [(i, i ^ s) for i in range(replicas)])
            for array, s in zip(arrays, range(replicas - 1, 0, -1))
        ]

    half = shape((slots // 2, width), F32)
    kept, sent, onehot, held, feature_rows, neighbour_rows = call(
        functools.partial(outgoing_kernel, towers, capacity),
        "outgoing",
        [],
        [
            half,
            half,
            shape((slots, rows), BF16),
            shape((slots, rows), F32),
            shape((rows, width), BF16),
            shape((fanout, rows), jnp.int32),
        ],
        [
            jnp.swapaxes(send_rows[0, 0], 0, 1),
            send_counts[0],
            features[0],
            jnp.swapaxes(neighbours[0], 0, 1),
        ],
        (
            pltpu.SMEM((capacity, groups), jnp.int32),
            pltpu.SMEM((1, groups), jnp.int32),
            pltpu.SemaphoreType.DMA((4,)),
        ),
    )
    arrived = swap_core(sent)
    own, far, far_turned, start = call(
        functools.partial(adjacency_kernel, towers, capacity),
        "adjacency",
        [held, feature_rows, neighbour_rows],
        [
            shape((rows, rows), BF16),
            shape((slots, rows), BF16),
            shape((rows, slots), BF16),
            shape((rows, width), F32),
        ],
    )
    near, *far_sent = call(
        functools.partial(hop_kernel, capacity),
        "halo_hop",
        [far, kept, arrived],
        [shape((2 * capacity, width), BF16)] + [shape((4 * capacity, width), BF16)] * passes,
    )
    far_halo = swap_far(far_sent)
    near = swap_near(near)
    passed = swap_core(
        call(
            functools.partial(pass_kernel, capacity),
            "halo_pass",
            far_halo,
            shape((2 * capacity * passes, width), BF16),
        )
    )
    candidate_rows, noise, weight, marks = call(
        prepare_kernel,
        "prepare",
        [],
        [
            shape((queries, cands), jnp.int32),
            shape((noise_rows, LANES), F32),
            shape((width, width), BF16),
            shape((DIGIT * queries, cands), BF16),
        ],
        [candidates[0], noise, weight],
        (pltpu.VMEM((noise_rows, LANES), F32), pltpu.SemaphoreType.DMA((3,))),
    )
    kept_turned, sent, d_pre = call(
        functools.partial(main_kernel, towers, capacity, fanout),
        "forward_backward",
        [far_turned, start, candidate_rows, noise, weight, marks, kept, arrived, *far_halo, passed, near],
        [
            shape((width // 2, rows), BF16),
            shape((width // 2, width), BF16),
            shape((rows, width), BF16),
        ],
    )

    arrived = swap_core(sent)
    kept = call(own_term_kernel, "own_term", [kept_turned, d_pre], shape((width // 2, width), F32))
    local, halo_kept, halo_sent = call(
        functools.partial(spread_kernel, towers, capacity, fanout),
        "spread",
        [d_pre, weight, own, far],
        [shape((rows, width), F32), half, half],
    )
    halo_arrived = swap_core(halo_sent)
    tall, wide = width // groups, width // replicas
    own_term, *terms = call(
        functools.partial(core_sum_kernel, replicas),
        "core_sum",
        [kept, arrived],
        [shape((width // 2, wide), F32)] + [shape((width // 2, wide), BF16)] * (replicas - 1),
    )
    terms = swap_replica(terms)

    def block(tiles, slot_count, dtype):
        return shape((-(-tiles * tall // 16) * 16 + slot_count * capacity * parts, LANES), dtype)

    own_tile, near, *far_sent = call(
        functools.partial(replica_sum_kernel, replicas, capacity),
        "replica_sum",
        [own_term, *terms, halo_kept, halo_arrived],
        [shape((tall, wide), F32), block(1, 2, BF16)] + [block(2, 4, BF16)] * passes,
    )
    far_sums = swap_far(far_sent)
    near = swap_near(near)
    passed = swap_core(
        call(
            functools.partial(pass_sums_kernel, capacity, parts, tall, wide),
            "pass_sums",
            far_sums,
            block(1, 2 * passes, BF16),
        )
    )
    d_features, weight_grad = call(
        functools.partial(final_kernel, capacity, devices),
        "final",
        [local, onehot, halo_kept, halo_arrived, own_tile, *far_sums, passed, near],
        [shape((rows, width), BF16), shape((tall, wide), F32)],
    )
    return (d_features[None], weight_grad)


def solution(mesh):
    groups, replicas = mesh.devices.shape
    split = jax.sharding.Mesh(
        mesh.devices.reshape(groups // 2, 2, replicas), ("z", "core", "replica")
    )
    graph = ("z", "core")
    placed = (
        P("replica", graph, None),
        P("replica", graph, None),
        P("replica", graph, None, None),
        P("replica", graph, None),
        P("replica", graph, None),
        P("replica", graph, None, None),
        P(),
    )
    return jax.shard_map(
        body,
        mesh=split,
        in_specs=placed,
        out_specs=(P("replica", graph, None), P(graph, "replica")),
        check_vma=False,
    )
```

```python
import functools
import math

import jax
import jax.numpy as jnp
from jax import lax
from jax.experimental import pallas as pl
from jax.experimental.pallas import tpu as pltpu
from jax.sharding import PartitionSpec as P

TOP = 20
SCORE_SCALE = 16.0
LOSS_SCALE = 16.0
EPSILON = 1e-05
LANES = 128
DIGIT = 16
F32 = jnp.float32
BF16 = jnp.bfloat16
NN = (((1,), (0,)), ((), ()))
TN = (((0,), (0,)), ((), ()))
NT = (((1,), (1,)), ((), ()))


def dot(a, b, dims):
    return lax.dot_general(a, b, dims, preferred_element_type=F32)


def slot_device(slot, towers):
    core = lax.axis_index("core")
    pair, e = slot // 2, slot % 2
    mixed = jnp.where(pair > 1, 1, 0)
    odd = pair % 2 * mixed
    upper = pair % 2 * (1 - mixed) + lax.bitwise_xor(core, odd) * mixed
    z = lax.bitwise_xor(lax.axis_index("z"), pair // 2 + upper * (towers // 2))
    return 2 * z + lax.bitwise_xor(core, lax.bitwise_xor(odd, jnp.int32(e)))


def kept_slots(towers):
    return [0, 2] + [4 * j + e for j in range(1, towers // 2) for e in range(2)]


def sent_slots(towers):
    return [1, 3] + [4 * j + 2 + e for j in range(1, towers // 2) for e in range(2)]


def slot_tiles(tiles):
    core = lax.axis_index("core")
    pairs = [xor_order(tiles[2 * z : 2 * z + 2], core) for z in range(len(tiles) // 2)]
    same = xor_order([pair[0] for pair in pairs], lax.axis_index("z"))
    other = xor_order([pair[1] for pair in pairs], lax.axis_index("z"))
    half = len(pairs) // 2
    ordered = [same[0], other[0], same[half], other[half]]
    for j in range(1, half):
        first = [xor_order([found[j], found[half + j]], core) for found in (same, other)]
        ordered += [first[0][0], first[1][0], first[1][1], first[0][1]]
    return ordered


def pick(array, slots, size):
    return jnp.concatenate([array[i * size : (i + 1) * size] for i in slots], axis=0)


def fold(rows):
    return jnp.concatenate(
        [rows[:, j : j + LANES] for j in range(0, rows.shape[1], LANES)], axis=0
    )


def unfold(block, parts):
    size = block.shape[0] // parts
    return jnp.concatenate([block[j * size : (j + 1) * size] for j in range(parts)], axis=1)


def near_rows(kept, arrived, size):
    return jnp.concatenate([pick(kept, [1], size), pick(arrived, [1], size)], axis=0)


def far_rows(kept, arrived, j, size):
    return jnp.concatenate([pick(x, [2 * j, 2 * j + 1], size) for x in (kept, arrived)], axis=0)


def slot_rows(kept, arrived, near, far, passed, size):
    rows = [pick(kept, [0], size), pick(arrived, [0], size), near]
    for j, block in enumerate(far):
        rows += [pick(block, [0, 2], size), pick(passed, [2 * j, 2 * j + 1], size)]
    return jnp.concatenate(rows, axis=0)


def xor_order(pieces, me):
    bit = 1
    while bit < len(pieces):
        swap = lax.bitwise_and(me, jnp.int32(bit)) != 0
        pieces = [jnp.where(swap, pieces[i ^ bit], pieces[i]) for i in range(len(pieces))]
        bit *= 2
    return pieces


def start_copies(pairs, sems):
    copies = [pltpu.make_async_copy(a, b, sems.at[i]) for i, (a, b) in enumerate(pairs)]
    for copy in copies:
        copy.start()
    return copies


def outgoing_kernel(
    towers,
    capacity,
    send_hbm,
    counts_hbm,
    features_hbm,
    neighbours_hbm,
    kept_ref,
    sent_ref,
    onehot_ref,
    held_ref,
    features_ref,
    neighbours_ref,
    send_smem,
    counts_smem,
    sems,
):
    copies = start_copies(
        [
            (send_hbm, send_smem),
            (counts_hbm, counts_smem),
            (features_hbm, features_ref),
            (neighbours_hbm, neighbours_ref),
        ],
        sems,
    )
    rows = features_ref.shape[0]
    slots = 2 * towers * capacity
    slot = lax.broadcasted_iota(jnp.int32, (slots, rows), 0)
    row = lax.broadcasted_iota(jnp.int32, (slots, rows), 1)
    named = jnp.full((slots, rows), -1, jnp.int32)
    held = jnp.zeros((slots, rows), jnp.int32)
    copies[0].wait()
    copies[1].wait()
    for i in range(2 * towers):
        device = slot_device(i, towers)
        held = jnp.where(slot // capacity == i, counts_smem[0, device], held)
        for k in range(capacity):
            named = jnp.where(slot == i * capacity + k, send_smem[k, device], named)
    onehot = (named == row).astype(F32).astype(BF16)
    onehot_ref[...] = onehot
    held_ref[...] = (slot % capacity < held).astype(F32)
    copies[2].wait()
    picked = dot(onehot, features_ref[...], NN)
    kept_ref[...] = pick(picked, kept_slots(towers), capacity)
    sent_ref[...] = pick(picked, sent_slots(towers), capacity)
    copies[3].wait()


def hop_kernel(capacity, after_ref, kept_ref, arrived_ref, near_ref, *far_refs):
    kept, arrived = kept_ref[...], arrived_ref[...]
    near_ref[...] = near_rows(kept, arrived, capacity).astype(BF16)
    for j, ref in enumerate(far_refs):
        ref[...] = far_rows(kept, arrived, j + 1, capacity).astype(BF16)


def pass_kernel(capacity, *refs):
    far_refs, out_ref = refs[:-1], refs[-1]
    rows = [pick(ref[...].astype(F32), [1, 3], capacity) for ref in far_refs]
    out_ref[...] = jnp.concatenate(rows, axis=0).astype(BF16)


def adjacency_kernel(
    towers,
    capacity,
    held_ref,
    features_ref,
    neighbours_ref,
    own_ref,
    far_ref,
    far_turned_ref,
    start_ref,
):
    rows = features_ref.shape[0]
    fanout = neighbours_ref.shape[0]
    slots = far_ref.shape[0]
    own = lax.broadcasted_iota(jnp.int32, (rows, rows), 0)
    far = lax.broadcasted_iota(jnp.int32, (slots, rows), 0)
    far_slot = slot_device(far // capacity, towers) * capacity + far % capacity + rows
    own_count = jnp.zeros((rows, rows), F32)
    far_count = jnp.zeros((slots, rows), F32)
    for f in range(fanout):
        named = neighbours_ref[f : f + 1, :]
        own_count = own_count + (own == named).astype(F32)
        far_count = far_count + (far_slot == named).astype(F32)
    own_count = own_count.astype(BF16)
    far_count = far_count * held_ref[...]
    far_ref[...] = far_count.astype(BF16)
    far_turned_ref[...] = far_count.T.astype(BF16)
    own_ref[...] = own_count
    features = features_ref[...]
    start_ref[...] = features.astype(F32) + dot(own_count, features, TN)


def prepare_kernel(
    candidates_hbm,
    noise_hbm,
    weight_hbm,
    candidates_ref,
    noise_ref,
    weight_ref,
    marks_ref,
    raw_noise_ref,
    sems,
):
    copies = start_copies(
        [(noise_hbm, raw_noise_ref), (weight_hbm, weight_ref), (candidates_hbm, candidates_ref)], sems
    )
    queries, cands = candidates_ref.shape
    blocks = cands // LANES
    samples = noise_ref.shape[0] // (queries * blocks)
    copies[0].wait()
    for m in range(samples):
        noise = [
            raw_noise_ref[pl.ds(j * samples + m, queries, stride=blocks * samples), :]
            for j in range(blocks)
        ]
        highest = jnp.max(functools.reduce(jnp.maximum, noise), axis=-1, keepdims=True)
        for j in range(blocks):
            at = (m * blocks + j) * queries
            noise_ref[at : at + queries, :] = jnp.exp(noise[j] - highest)
    copies[2].wait()
    low = lax.bitwise_and(candidates_ref[...], jnp.int32(DIGIT - 1))
    for digit in range(DIGIT):
        marks_ref[digit * queries : (digit + 1) * queries, :] = (
            (low == digit).astype(F32).astype(BF16)
        )
    copies[1].wait()


def main_kernel(
    towers,
    capacity,
    fanout,
    far_turned_ref,
    start_ref,
    candidates_ref,
    noise_ref,
    weight_ref,
    marks_ref,
    halo_kept_ref,
    halo_arrived_ref,
    *refs,
):
    *halo_refs, kept_turned_ref, sent_ref, d_pre_ref = refs
    *far_halo, passed, near = [ref[...].astype(F32) for ref in halo_refs]
    rows, width = start_ref.shape
    queries, cands = candidates_ref.shape
    samples = noise_ref.shape[0] // (queries * (cands // LANES))
    halo = slot_rows(halo_kept_ref[...], halo_arrived_ref[...], near, far_halo, passed, capacity)
    sums = start_ref[...] + dot(far_turned_ref[...], halo.astype(BF16), NN)
    mean_rows = (sums * (1.0 / (fanout + 1))).astype(BF16)

    tall = width // (2 * towers)
    turned = mean_rows.astype(F32).T
    tiles = slot_tiles([turned[i * tall : (i + 1) * tall] for i in range(2 * towers)])
    kept_turned, sent_turned = [
        jnp.concatenate([tiles[i] for i in slots], axis=0).astype(BF16)
        for slots in (kept_slots(towers), sent_slots(towers))
    ]

    weight = weight_ref[...]
    pre = dot(mean_rows, weight, NN)
    inverse = lax.rsqrt(jnp.mean(pre * pre, axis=-1, keepdims=True) + EPSILON)
    embedded = (pre * inverse).astype(BF16)
    factor = SCORE_SCALE / width
    rounded = pre.astype(BF16)
    similar = dot(rounded[:queries], rounded, NT)
    inverse_of_column = jnp.broadcast_to(inverse, (rows, rows)).T[:queries]
    similar = similar * (factor * inverse[:queries] * inverse_of_column)
    blocks = cands // LANES
    scores = [
        jnp.take_along_axis(similar, candidates_ref[:, j * LANES : (j + 1) * LANES], axis=1)
        for j in range(blocks)
    ]
    grown = [jnp.exp(x) for x in scores]
    soft = [jnp.zeros((queries, LANES), F32) for _ in range(blocks)]
    for m in range(samples):
        at = m * blocks * queries
        noise = [noise_ref[at + j * queries : at + (j + 1) * queries, :] for j in range(blocks)]
        total = jnp.sum(sum(n * g for n, g in zip(noise, grown)), axis=-1, keepdims=True)
        scale = (LOSS_SCALE * TOP / samples) / total
        soft = [a + n * scale for a, n in zip(soft, noise)]
    soft = [a * g for a, g in zip(soft, grown)]
    lane = lax.broadcasted_iota(jnp.int32, (queries, LANES), 1)
    d_scores = [
        jnp.where(lane + j * LANES < TOP, s - LOSS_SCALE, s) if j * LANES < TOP else s
        for j, s in enumerate(soft)
    ]
    d_scores = jnp.concatenate(d_scores, axis=1)

    high = candidates_ref[...] // DIGIT
    digits = rows // DIGIT
    weighted = [jnp.where(high == digit, d_scores, 0.0) for digit in range(digits)]
    crossed = dot(marks_ref[...], jnp.concatenate(weighted, axis=0).astype(BF16), NT)
    q_row = lax.broadcasted_iota(jnp.int32, crossed.shape, 0) % queries
    q_column = lax.broadcasted_iota(jnp.int32, crossed.shape, 1) % queries
    crossed = jnp.where(q_row == q_column, crossed, 0.0)
    kept = jnp.sum(crossed.reshape(DIGIT, queries, digits * queries), axis=1)
    d_similar = jnp.concatenate(
        [kept[:, i * queries : (i + 1) * queries] for i in range(digits)], axis=0
    ).astype(BF16)

    d_embedded = factor * dot(d_similar, embedded[:queries], NN)
    d_queries = factor * dot(d_similar, embedded, TN)
    d_embedded = jnp.concatenate(
        [d_embedded[:queries] + d_queries, d_embedded[queries:]], axis=0
    )
    inner = jnp.mean(d_embedded * pre, axis=-1, keepdims=True)
    d_pre = (inverse * d_embedded - inverse * inverse * inverse * pre * inner).astype(BF16)

    d_pre_ref[...] = d_pre
    sent_ref[...] = dot(sent_turned, d_pre, NN).astype(BF16)
    kept_turned_ref[...] = kept_turned


def own_term_kernel(kept_turned_ref, d_pre_ref, out_ref):
    out_ref[...] = dot(kept_turned_ref[...], d_pre_ref[...], NN)


def spread_kernel(
    towers, capacity, fanout, d_pre_ref, weight_ref, own_ref, far_ref, local_ref, kept_ref, sent_ref
):
    share = (dot(d_pre_ref[...], weight_ref[...], NT) * (1.0 / (fanout + 1))).astype(BF16)
    halo_grad = dot(far_ref[...], share, NN)
    kept_ref[...] = pick(halo_grad, kept_slots(towers), capacity)
    sent_ref[...] = pick(halo_grad, sent_slots(towers), capacity)
    local_ref[...] = share.astype(F32) + dot(own_ref[...], share, NN)


def core_sum_kernel(replicas, kept_ref, arrived_ref, own_ref, *out_refs):
    total = kept_ref[...] + arrived_ref[...].astype(F32)
    wide = total.shape[1] // replicas
    pieces = [total[:, r * wide : (r + 1) * wide] for r in range(replicas)]
    pieces = xor_order(pieces, lax.axis_index("replica"))
    own_ref[...] = pieces[0]
    for ref, piece in zip(out_refs, pieces[:0:-1]):
        ref[...] = piece.astype(BF16)


def store_block(ref, tiles, rows):
    high, wide = tiles.shape
    block = fold(rows)
    if (high + block.shape[0], wide) != ref.shape:
        ref[...] = jnp.zeros(ref.shape, ref.dtype)
    ref[0:high, 0:wide] = tiles.astype(ref.dtype)
    ref[ref.shape[0] - block.shape[0] :, :] = block.astype(ref.dtype)


def load_block(ref, high, wide, slots, parts):
    block = ref[...].astype(F32)
    return block[:high, :wide], unfold(block[block.shape[0] - slots * parts :], parts)


def replica_sum_kernel(replicas, capacity, *refs):
    term_refs, refs = refs[:replicas], refs[replicas:]
    kept_ref, arrived_ref, own_ref, near_ref, *far_refs = refs
    total = sum(ref[...].astype(F32) for ref in term_refs)
    tall = own_ref.shape[0]
    kept, arrived = kept_ref[...], arrived_ref[...]
    own_ref[...] = total[:tall]
    store_block(near_ref, total[tall : 2 * tall], near_rows(kept, arrived, capacity))
    for j, ref in enumerate(far_refs):
        tiles = total[2 * (j + 1) * tall : 2 * (j + 2) * tall]
        store_block(ref, tiles, far_rows(kept, arrived, j + 1, capacity))


def pass_sums_kernel(capacity, parts, tall, wide, *refs):
    far_refs, out_ref = refs[:-1], refs[-1]
    loaded = [load_block(ref, 2 * tall, wide, 4 * capacity, parts) for ref in far_refs]
    store_block(
        out_ref,
        sum(tiles[tall:] for tiles, _ in loaded),
        jnp.concatenate([pick(rows, [1, 3], capacity) for _, rows in loaded], axis=0),
    )


def final_kernel(capacity, devices, local_ref, onehot_ref, kept_ref, arrived_ref, own_ref, *refs):
    *far_refs, passed_ref, near_ref, features_out, weight_out = refs
    tall, wide = own_ref.shape
    parts = local_ref.shape[1] // LANES
    near_tile, near = load_block(near_ref, tall, wide, 2 * capacity, parts)
    loaded = [load_block(ref, 2 * tall, wide, 4 * capacity, parts) for ref in far_refs]
    passed_tile, passed = load_block(passed_ref, tall, wide, 2 * capacity * len(far_refs), parts)
    returned = slot_rows(
        kept_ref[...], arrived_ref[...], near, [rows for _, rows in loaded], passed, capacity
    )
    features_out[...] = (local_ref[...] + dot(onehot_ref[...], returned.astype(BF16), TN)).astype(BF16)
    total = own_ref[...] + near_tile + passed_tile + sum(tiles[:tall] for tiles, _ in loaded)
    weight_out[...] = total * (1.0 / math.sqrt(devices))


def body(features, neighbours, send_rows, send_counts, candidates, perturbation, weight):
    towers = lax.axis_size("z")
    replicas = lax.axis_size("replica")
    groups = 2 * towers
    devices = groups * replicas
    capacity = send_rows.shape[3]
    _, rows, width = features.shape
    _, queries, samples, cands = perturbation.shape
    fanout = neighbours.shape[2]
    slots = groups * capacity
    parts = width // LANES
    passes = towers // 2 - 1
    noise_rows = queries * samples * (cands // LANES)
    noise = (
        perturbation.reshape(queries, samples, cands // LANES, LANES)
        .transpose(0, 2, 1, 3)
        .reshape(noise_rows, LANES)
    )
    hbm = pl.BlockSpec(memory_space=pltpu.HBM)
    vmem = pl.BlockSpec(memory_space=pltpu.VMEM)
    shape = jax.ShapeDtypeStruct

    def call(kernel, name, operands, out_shape, from_hbm=(), scratch=()):
        from_hbm = [pltpu.with_memory_space_constraint(x, pltpu.HBM) for x in from_hbm]
        return pl.pallas_call(
            kernel,
            out_shape=out_shape,
            in_specs=[hbm] * len(from_hbm) + [vmem] * len(operands),
            out_specs=jax.tree.map(lambda _: vmem, out_shape),
            scratch_shapes=scratch,
            compiler_params=pltpu.CompilerParams(vmem_limit_bytes=32 * 1024 * 1024),
            name=name,
        )(*from_hbm, *operands)

    def swap_core(array):
        return lax.ppermute(array, "core", [(0, 1), (1, 0)])

    def swap_near(array):
        return lax.ppermute(array, "z", [(i, i ^ towers // 2) for i in range(towers)])

    def swap_far(arrays):
        return [
            lax.ppermute(
                array,
                ("z", "core"),
                [(2 * i + c, 2 * (i ^ j + c * towers // 2) + c) for i in range(towers) for c in range(2)],
            )
            for j, array in enumerate(arrays, 1)
        ]

    def swap_replica(arrays):
        return [
            lax.ppermute(array, "replica", [(i, i ^ s) for i in range(replicas)])
            for array, s in zip(arrays, range(replicas - 1, 0, -1))
        ]

    half = shape((slots // 2, width), F32)
    kept, sent, onehot, held, feature_rows, neighbour_rows = call(
        functools.partial(outgoing_kernel, towers, capacity),
        "outgoing",
        [],
        [
            half,
            half,
            shape((slots, rows), BF16),
            shape((slots, rows), F32),
            shape((rows, width), BF16),
            shape((fanout, rows), jnp.int32),
        ],
        [
            jnp.swapaxes(send_rows[0, 0], 0, 1),
            send_counts[0],
            features[0],
            jnp.swapaxes(neighbours[0], 0, 1),
        ],
        (
            pltpu.SMEM((capacity, groups), jnp.int32),
            pltpu.SMEM((1, groups), jnp.int32),
            pltpu.SemaphoreType.DMA((4,)),
        ),
    )
    arrived = swap_core(sent)
    own, far, far_turned, start = call(
        functools.partial(adjacency_kernel, towers, capacity),
        "adjacency",
        [held, feature_rows, neighbour_rows],
        [
            shape((rows, rows), BF16),
            shape((slots, rows), BF16),
            shape((rows, slots), BF16),
            shape((rows, width), F32),
        ],
    )
    near, *far_sent = call(
        functools.partial(hop_kernel, capacity),
        "halo_hop",
        [far, kept, arrived],
        [shape((2 * capacity, width), BF16)] + [shape((4 * capacity, width), BF16)] * passes,
    )
    far_halo = swap_far(far_sent)
    near = swap_near(near)
    passed = swap_core(
        call(
            functools.partial(pass_kernel, capacity),
            "halo_pass",
            far_halo,
            shape((2 * capacity * passes, width), BF16),
        )
    )
    candidate_rows, noise, weight, marks = call(
        prepare_kernel,
        "prepare",
        [],
        [
            shape((queries, cands), jnp.int32),
            shape((noise_rows, LANES), F32),
            shape((width, width), BF16),
            shape((DIGIT * queries, cands), BF16),
        ],
        [candidates[0], noise, weight],
        (pltpu.VMEM((noise_rows, LANES), F32), pltpu.SemaphoreType.DMA((3,))),
    )
    kept_turned, sent, d_pre = call(
        functools.partial(main_kernel, towers, capacity, fanout),
        "forward_backward",
        [far_turned, start, candidate_rows, noise, weight, marks, kept, arrived, *far_halo, passed, near],
        [
            shape((width // 2, rows), BF16),
            shape((width // 2, width), BF16),
            shape((rows, width), BF16),
        ],
    )

    arrived = swap_core(sent)
    kept = call(own_term_kernel, "own_term", [kept_turned, d_pre], shape((width // 2, width), F32))
    local, halo_kept, halo_sent = call(
        functools.partial(spread_kernel, towers, capacity, fanout),
        "spread",
        [d_pre, weight, own, far],
        [shape((rows, width), F32), half, half],
    )
    halo_arrived = swap_core(halo_sent)
    tall, wide = width // groups, width // replicas
    own_term, *terms = call(
        functools.partial(core_sum_kernel, replicas),
        "core_sum",
        [kept, arrived],
        [shape((width // 2, wide), F32)] + [shape((width // 2, wide), BF16)] * (replicas - 1),
    )
    terms = swap_replica(terms)

    def block(tiles, slot_count, dtype):
        return shape((-(-tiles * tall // 16) * 16 + slot_count * capacity * parts, LANES), dtype)

    own_tile, near, *far_sent = call(
        functools.partial(replica_sum_kernel, replicas, capacity),
        "replica_sum",
        [own_term, *terms, halo_kept, halo_arrived],
        [shape((tall, wide), F32), block(1, 2, BF16)] + [block(2, 4, BF16)] * passes,
    )
    far_sums = swap_far(far_sent)
    near = swap_near(near)
    passed = swap_core(
        call(
            functools.partial(pass_sums_kernel, capacity, parts, tall, wide),
            "pass_sums",
            far_sums,
            block(1, 2 * passes, BF16),
        )
    )
    d_features, weight_grad = call(
        functools.partial(final_kernel, capacity, devices),
        "final",
        [local, onehot, halo_kept, halo_arrived, own_tile, *far_sums, passed, near],
        [shape((rows, width), BF16), shape((tall, wide), F32)],
    )
    return (d_features[None], weight_grad)


def solution(mesh):
    groups, replicas = mesh.devices.shape
    split = jax.sharding.Mesh(
        mesh.devices.reshape(groups // 2, 2, replicas), ("z", "core", "replica")
    )
    graph = ("z", "core")
    placed = (
        P("replica", graph, None),
        P("replica", graph, None),
        P("replica", graph, None, None),
        P("replica", graph, None),
        P("replica", graph, None),
        P("replica", graph, None, None),
        P(),
    )
    return jax.shard_map(
        body,
        mesh=split,
        in_specs=placed,
        out_specs=(P("replica", graph, None), P(graph, "replica")),
        check_vma=False,
    )
```
